32 devices in a mesh: row: 8 (over y, x, core), col: 4 (over z).
Axes of the slice: x: 2, y: 2, z: 4, core: 2. Of those that a mesh axis runs over, the one named last changes fastest.
Arguments:
- diag_blocks: bfloat16 [256, 128, 128], P(('row', 'col')), may hold values from -0.03 to 3, as said below
- off_blocks: bfloat16 [256, 6, 128, 128], P(('row', 'col')), may hold values from -0.375 to 0.375
- neighbors: int32 [256, 6], P(('row', 'col')), may hold values from -1 to 255, as said below
- levels: int32 [256], P(('row', 'col')), may hold values from 0 to 1, as said below
Outputs:
- pivot_inverse: bfloat16 [256, 128, 128], P(('row', 'col'))
- factor_blocks: bfloat16 [256, 6, 128, 128], P(('row', 'col'))
The draws below stay inside these ranges and needn't reach their ends.
Inputs may be any that keep to these rules, and one draw needn't show every extreme that they name: `levels`: block row i lies on device number d = i // 8, where d = r * (number of devices along col) + c for the device with index r along row and index c along col. On each device the rows of level 0 come first; a device holds between 2 and 6 rows of level 0, and in every draw some device holds exactly 6 and some exactly 2. `neighbors`: A live slot names a row of the other level. Slot 0 names a row on the device whose row index is one higher, slot 1 one lower, slot 2 on the device whose col index is one higher, slot 3 one lower, slots 4 and 5 on the same device. If row i names row j in slot k, row j names row i in slot (1, 0, 3, 2, 5, 4)[k]. `diag_blocks`: diagonal entries from 1 to 3; off-diagonal entries of either sign, each row's sum of their magnitudes under 0.9 times that row's diagonal entry.
All inputs are finite; a program needn't handle non-finite values.
Results may differ from the reference program's by a relative error of at most 0.0053.
Values may be sent and summed in bfloat16 or wider, within the bound.
No kernel may reach another device: no remote copies, remote signals or barrier semaphores. Data moves between devices by JAX's collectives and lax.ppermute only.
A program may use at most 64 MiB of HBM per device.

```python
import math
import jax
import jax.numpy as jnp
import numpy as np
from jax import lax

B = 128
K = 6
NB = 8
NS_STEPS = 4
CAP = 6
NROWS = 256
N_ROW = 8
N_COL = 4


MOVES = ((1, 0), (-1, 0), (0, 1), (0, -1), (0, 0), (0, 0))


def slot_pattern(key):
    base = jax.random.fold_in(key, 913)
    count_key, pick_key, shift_key = jax.random.split(base, 3)
    devices_all = N_ROW * N_COL
    lowest = NB - CAP
    counts = jax.random.randint(count_key, (devices_all,), lowest, CAP + 1)
    chosen = jax.random.permutation(pick_key, devices_all)
    counts = counts.at[chosen[0]].set(CAP).at[chosen[1]].set(lowest)
    shifts = jax.random.randint(shift_key, (K, devices_all), 0, 3)
    device = jnp.arange(devices_all, dtype=jnp.int32)[:, None]
    position = jnp.arange(NB, dtype=jnp.int32)[None, :]
    early_count = counts[:, None]
    level_table = (position >= early_count).astype(jnp.int32)
    grid_row = device // N_COL
    grid_col = device % N_COL
    columns = []
    for slot_index in range(K):
        step_row, step_col = MOVES[slot_index]
        target_row = grid_row + step_row
        target_col = grid_col + step_col
        inside = (target_row >= 0) & (target_row < N_ROW) & (target_col >= 0) & (target_col < N_COL)
        target = jnp.clip(target_row, 0, N_ROW - 1) * N_COL + jnp.clip(target_col, 0, N_COL - 1)
        target_count = counts[target]
        late_rank = position - early_count + shifts[slot_index][device]
        late_ok = inside & (late_rank < target_count)
        late_value = target * NB + late_rank
        early_rank = position - shifts[slot_index ^ 1][target]
        early_ok = inside & (early_rank >= 0) & (early_rank < NB - target_count)
        early_value = target * NB + target_count + early_rank
        value = jnp.where(level_table == 1, jnp.where(late_ok, late_value, -1), jnp.where(early_ok, early_value, -1))
        columns.append(value)
    named = jnp.stack(columns, axis=-1).reshape(NROWS, K).astype(jnp.int32)
    return (level_table.reshape(NROWS).astype(jnp.int32), named)


def draw_levels(key, part):
    return slot_pattern(key)[0]


def draw_neighbors(key, part):
    return slot_pattern(key)[1]


def draw_diag_blocks(key, part):
    scale_key, spread_key, sign_key = jax.random.split(jax.random.fold_in(key, 5), 3)
    diagonal = jnp.exp(jax.random.uniform(scale_key, (NROWS, B), minval=0.0, maxval=math.log(3.0)))
    spread = jax.random.uniform(spread_key, (NROWS, B, B), minval=0.4, maxval=1.0)
    signs = jnp.where(jax.random.uniform(sign_key, (NROWS, B, B)) < 0.5, -1.0, 1.0)
    identity = jnp.eye(B, dtype=jnp.float32)
    denominator = max(B, 128) - 1
    coupling = diagonal[:, :, None] * signs * spread * (0.85 / denominator)
    matrix = coupling * (1.0 - identity) + diagonal[:, :, None] * identity
    return matrix.astype(jnp.bfloat16)


def level_of(key, extent, pieces, low, largest):
    gain = 1.0
    for dim, parts in pieces:
        heights = jax.random.uniform(jax.random.fold_in(jax.random.fold_in(key, 6), dim), (parts,), jnp.float32, low / len(pieces), largest / len(pieces))
        gain = gain * jnp.repeat(jnp.exp(heights), extent[dim] // parts).reshape((-1,) + (1,) * (len(extent) - 1 - dim))
    return gain


def normal_values(rng, shape, scale, bound, cuts=(), kind=jnp.bfloat16):
    values = jax.random.normal(rng, shape, jnp.float32) * scale
    if len(cuts) > 0:
        values = level_of(rng, shape, cuts, -0.22, 0.18) * values
    return jnp.clip(values, min=-bound, max=bound).astype(kind)


def setup_inputs(seed: int = 0) -> dict:
    splits = jax.random.split(jax.random.key(seed), 5)
    diag_blocks = draw_diag_blocks(jax.random.fold_in(splits[4], 71), 0)
    off_blocks = normal_values(splits[1], (NROWS, K, B, B), 0.025, 0.375, ((0, 32),))
    neighbors = draw_neighbors(jax.random.fold_in(splits[4], 71), 0)
    levels = draw_levels(jax.random.fold_in(splits[4], 71), 0)
    return dict(diag_blocks=diag_blocks, off_blocks=off_blocks, neighbors=neighbors, levels=levels)


MIRROR_TABLE = np.array([1, 0, 3, 2, 5, 4], dtype=np.int32)


def approx_inverse(matrix):
    magnitude = jnp.abs(matrix)
    column_norm = jnp.max(jnp.sum(magnitude, axis=1), axis=1)
    row_norm = jnp.max(jnp.sum(magnitude, axis=2), axis=1)
    iterate = jnp.swapaxes(matrix, 1, 2) / (column_norm * row_norm)[:, None, None]
    for step_index in range(NS_STEPS):
        product = jnp.einsum('nij,njk->nik', matrix, iterate, precision=lax.Precision.HIGHEST)
        iterate = 2.0 * iterate - jnp.einsum('nij,njk->nik', iterate, product, precision=lax.Precision.HIGHEST)
    return iterate


def reference(diag_blocks, off_blocks, neighbors, levels):
    groups = NROWS // NB
    active = neighbors >= 0

    def first_pass(items):
        diag_group, off_group, active_group = items
        inverse = approx_inverse(diag_group.astype(jnp.float32)).astype(jnp.bfloat16)
        scaled = jnp.einsum('nij,nkjl->nkil', inverse.astype(jnp.float32), off_group.astype(jnp.float32))
        scaled = jnp.where(active_group[:, :, None, None], scaled, 0.0).astype(jnp.bfloat16)
        return inverse, scaled

    inverses, scaled_rows = lax.map(first_pass, (diag_blocks.reshape(groups, NB, B, B), off_blocks.reshape(groups, NB, K, B, B), active.reshape(groups, NB, K)))
    inverses = inverses.reshape(NROWS, B, B)
    scaled_rows = scaled_rows.reshape(NROWS, K, B, B)
    mirror = jnp.asarray(MIRROR_TABLE)

    def second_pass(items):
        diag_group, off_group, named_group, level_group = items
        active_group = named_group >= 0
        target = jnp.where(active_group, named_group, 0).astype(jnp.int32)
        across = inverses[target].astype(jnp.float32)
        facing = scaled_rows[target, mirror[None, :]].astype(jnp.float32)
        lower_blocks = jnp.where(active_group[:, :, None, None], off_group.astype(jnp.float32), 0.0)
        lower_factor = jnp.einsum('qkij,qkjl->qkil', lower_blocks, across).astype(jnp.bfloat16)
        schur = jnp.einsum('qkij,qkjl->qil', lower_blocks, facing)
        diag_float = diag_group.astype(jnp.float32)
        later = (level_group == 1)[:, None, None]
        pivot = jnp.where(later, diag_float - schur, diag_float)
        return approx_inverse(pivot).astype(jnp.bfloat16), lower_factor

    pivots, lowers = lax.map(second_pass, (diag_blocks.reshape(groups, NB, B, B), off_blocks.reshape(groups, NB, K, B, B), neighbors.reshape(groups, NB, K), levels.reshape(groups, NB)))
    lowers = lowers.reshape(NROWS, K, B, B)
    factor = jnp.where((levels == 0)[:, None, None, None], scaled_rows, lowers)
    return pivots.reshape(NROWS, B, B), factor
```

```python
import functools
import jax
import jax.numpy as jnp
from jax import lax
from jax.experimental import pallas as pl
from jax.experimental.pallas import tpu as pltpu
from jax.sharding import PartitionSpec as P

NS_STEPS = 4
MIRROR = (1, 0, 3, 2, 5, 4)
VMEM_LIMIT = 40 * 1024 * 1024
REMOTE = 4
PAIRS = (("col", 1), ("col", 0), ("row", 1), ("row", 0))


def pair_list(size, odd):
    lower = [(i, i + 1) for i in range(odd, size - 1, 2)]
    return lower + [(j, i) for i, j in lower]


def dot(a, b):
    return jnp.dot(a, b, preferred_element_type=jnp.float32)


def dot_t(a, b):
    return lax.dot_general(a, b, (((1,), (1,)), ((), ())), preferred_element_type=jnp.float32)


def halves(value):
    high = value.astype(jnp.bfloat16)
    low = (value - high.astype(jnp.float32)).astype(jnp.bfloat16)
    return high, low


def approx_inverses(matrices, exact):
    size = matrices[0].shape[0]
    eye = (
        lax.broadcasted_iota(jnp.int32, (size, size), 0)
        == lax.broadcasted_iota(jnp.int32, (size, size), 1)
    ).astype(jnp.float32)
    iterates, residuals = [], []
    for matrix in matrices:
        turned = matrix.T
        column = jnp.max(jnp.sum(jnp.abs(matrix), axis=0, keepdims=True), axis=1, keepdims=True)
        row = jnp.max(jnp.sum(jnp.abs(turned), axis=0, keepdims=True), axis=1, keepdims=True)
        scale = 1.0 / (column * row)
        if exact:
            square = dot_t(matrix.astype(jnp.bfloat16), matrix.astype(jnp.bfloat16))
        else:
            high, low = halves(matrix)
            left = jnp.concatenate([high, low], axis=1)
            right = jnp.concatenate(
                [
                    jnp.concatenate([high, high], axis=1),
                    jnp.concatenate([low, low], axis=1),
                ],
                axis=0,
            )
            both = dot_t(left, right)
            square = both[:, :size] + both[:, size:]
        iterates.append(turned * scale)
        residuals.append(eye - square * scale)
    for step in range(NS_STEPS):
        last = step == NS_STEPS - 1
        for n in range(len(matrices)):
            r_high, r_low = halves(residuals[n])
            x_high, x_low = halves(iterates[n])
            row = jnp.concatenate([r_high, r_low], axis=1)
            right = jnp.concatenate([row, row], axis=0)
            left = jnp.concatenate([x_high, x_low], axis=1)
            if not last:
                left = jnp.concatenate([left, row], axis=0)
            both = dot(left, right)
            both = both[:, :size] + both[:, size:]
            iterates[n] = iterates[n] + both[:size]
            if not last:
                residuals[n] = both[size:]
    return iterates


def slot_order():
    row = lax.axis_index("row") % 2
    col = lax.axis_index("col") % 2
    return (3 - col, 2 + col, 1 - row, row)


def first_kernel(capacity, diag_hbm, off_hbm, *rest):
    payloads, (inverse, diag, off, sems) = rest[:REMOTE], rest[REMOTE:]
    slots = slot_order()
    copy_diag = pltpu.make_async_copy(diag_hbm.at[pl.ds(0, capacity)], diag, sems.at[0])
    copy_off = pltpu.make_async_copy(off_hbm.at[pl.ds(0, capacity), pl.ds(0, REMOTE)], off, sems.at[1])
    copy_diag.start()
    copy_off.start()
    copy_diag.wait()
    inverses = approx_inverses([diag[n].astype(jnp.float32) for n in range(capacity)], True)
    inverses = [value.astype(jnp.bfloat16) for value in inverses]
    copy_off.wait()
    for n in range(capacity):
        inverse[n] = inverses[n]
        for j in range(0, REMOTE, 2):
            scaled = dot(inverses[n], jnp.concatenate([off[n, slots[j]], off[n, slots[j + 1]]], axis=1))
            for i in range(2):
                payloads[j + i][n] = inverses[n]
                payloads[j + i][capacity + n] = scaled[:, i * 128 : (i + 1) * 128].astype(jnp.bfloat16)


def local_kernel(
    capacity, rows, neighbors, levels, off_hbm, inverse, p0, p1, p2, p3,
    factor_hbm, schur, lower, scaled, off, nothing, sems,
):
    payloads = (p0, p1, p2, p3)
    slots = slot_order()
    start = rows - capacity
    copy_off = pltpu.make_async_copy(off_hbm.at[:, pl.ds(REMOTE, 2)], off, sems.at[0])
    copy_off.start()
    nothing[...] = jnp.zeros_like(nothing)

    def each_remote(act):
        for n in range(capacity):

            @pl.when(levels[n] == 0)
            def _():
                for j in range(REMOTE):
                    target = factor_hbm.at[n, slots[j]]

                    @pl.when(neighbors[n, slots[j]] >= 0)
                    def _():
                        act(pltpu.make_async_copy(payloads[j].at[capacity + n], target, sems.at[1]))

                    @pl.when(neighbors[n, slots[j]] < 0)
                    def _():
                        act(pltpu.make_async_copy(nothing, target, sems.at[1]))

    each_remote(lambda c: c.start())
    copy_off.wait()
    for n in range(capacity):
        both = dot(inverse[n], jnp.concatenate([off[n, 0], off[n, 1]], axis=1))
        for i in range(2):
            part = both[:, i * 128 : (i + 1) * 128]
            part = jnp.where(neighbors[n, REMOTE + i] >= 0, part, 0.0)
            scaled[n, i] = part.astype(jnp.bfloat16)

    def local_row(t, carry):
        q = start + t
        total = None
        for i in range(2):
            named = neighbors[q, REMOTE + i]
            place = jnp.clip(named % rows, 0, capacity - 1)
            block = jnp.where(named >= 0, off[q, i].astype(jnp.float32), 0.0).astype(jnp.bfloat16)
            both = dot(block, jnp.concatenate([inverse[place], scaled[place, 1 - i]], axis=1))
            lower[t, i] = both[:, :128].astype(jnp.bfloat16)
            total = both[:, 128:] if total is None else total + both[:, 128:]
        schur[t] = total
        return carry

    lax.fori_loop(0, capacity, local_row, 0)

    def each_local(act):
        for n in range(rows):
            target = factor_hbm.at[n, pl.ds(REMOTE, 2)]
            if n < capacity:

                @pl.when(levels[n] == 0)
                def _():
                    act(pltpu.make_async_copy(scaled.at[n], target, sems.at[2]))

            if n >= start:

                @pl.when(levels[n] == 1)
                def _():
                    act(pltpu.make_async_copy(lower.at[n - start], target, sems.at[2]))

    each_local(lambda c: c.start())
    each_remote(lambda c: c.wait())
    each_local(lambda c: c.wait())


def second_kernel(
    capacity, rows, neighbors, levels, diag_hbm, off_hbm, factor_in, inverse, r0, r1, r2, r3, schur,
    pivot, factor_hbm, diag, off, lower, sems,
):
    del factor_in
    received = (r0, r1, r2, r3)
    slots = slot_order()
    start = rows - capacity
    copy_diag = pltpu.make_async_copy(diag_hbm.at[pl.ds(start, capacity)], diag, sems.at[0])
    copy_off = pltpu.make_async_copy(off_hbm.at[pl.ds(start, capacity), pl.ds(0, REMOTE)], off, sems.at[1])
    copy_diag.start()
    copy_off.start()
    copy_diag.wait()
    copy_off.wait()
    pivots = []
    for t in range(capacity):
        q = start + t
        total = schur[t]
        for j in range(REMOTE):
            slot = slots[j]
            named = neighbors[q, slot]
            place = jnp.clip(named % rows, 0, capacity - 1)
            block = jnp.where(named >= 0, off[t, slot].astype(jnp.float32), 0.0).astype(jnp.bfloat16)
            both = dot(block, jnp.concatenate([received[j][place], received[j][capacity + place]], axis=1))
            lower[t, slot] = both[:, :128].astype(jnp.bfloat16)
            total = total + both[:, 128:]
        pivots.append(diag[t].astype(jnp.float32) - total)

    def each_lower(act):
        for t in range(capacity):

            @pl.when(levels[start + t] == 1)
            def _():
                act(pltpu.make_async_copy(lower.at[t], factor_hbm.at[start + t, pl.ds(0, REMOTE)], sems.at[2]))

    each_lower(lambda c: c.start())
    inverses = approx_inverses(pivots, False)
    for n in range(rows):
        if n < start:
            pivot[n] = inverse[n]
        elif n >= capacity:
            pivot[n] = inverses[n - start].astype(jnp.bfloat16)
        else:
            pivot[n] = jnp.where(
                levels[n] == 0, inverse[n].astype(jnp.float32), inverses[n - start]
            ).astype(jnp.bfloat16)
    each_lower(lambda c: c.wait())


def shards(diag_blocks, off_blocks, neighbors, levels):
    rows, slots = off_blocks.shape[:2]
    size = diag_blocks.shape[1]
    capacity = 3 * rows // 4
    smem = pl.BlockSpec(memory_space=pltpu.SMEM)
    vmem = pl.BlockSpec(memory_space=pltpu.VMEM)
    hbm = pl.BlockSpec(memory_space=pltpu.HBM)
    params = pltpu.CompilerParams(vmem_limit_bytes=VMEM_LIMIT)
    bf16 = jnp.bfloat16
    payload = jax.ShapeDtypeStruct((2 * capacity, size, size), bf16)

    diag_blocks = pltpu.with_memory_space_constraint(diag_blocks, pltpu.HBM)
    off_blocks = pltpu.with_memory_space_constraint(off_blocks, pltpu.HBM)
    *payloads, inverse = pl.pallas_call(
        functools.partial(first_kernel, capacity),
        out_shape=[payload] * REMOTE + [jax.ShapeDtypeStruct((capacity, size, size), bf16)],
        in_specs=[hbm, hbm],
        out_specs=[vmem] * (REMOTE + 1),
        scratch_shapes=[
            pltpu.VMEM((capacity, size, size), bf16),
            pltpu.VMEM((capacity, REMOTE, size, size), bf16),
            pltpu.SemaphoreType.DMA((2,)),
        ],
        compiler_params=params,
        name="first_inverses",
    )(diag_blocks, off_blocks)

    received = []
    for j, (axis, odd) in enumerate(PAIRS):
        received.append(lax.ppermute(payloads[j], axis, pair_list(lax.axis_size(axis), odd)))

    factor, schur = pl.pallas_call(
        functools.partial(local_kernel, capacity, rows),
        out_shape=[
            jax.ShapeDtypeStruct((rows, slots, size, size), bf16),
            jax.ShapeDtypeStruct((capacity, size, size), jnp.float32),
        ],
        in_specs=[smem, smem, hbm] + [vmem] * (REMOTE + 1),
        out_specs=[hbm, vmem],
        scratch_shapes=[
            pltpu.VMEM((capacity, 2, size, size), bf16),
            pltpu.VMEM((capacity, 2, size, size), bf16),
            pltpu.VMEM((rows, 2, size, size), bf16),
            pltpu.VMEM((size, size), bf16),
            pltpu.SemaphoreType.DMA((3,)),
        ],
        compiler_params=params,
        cost_estimate=pl.CostEstimate(flops=400_000_000, bytes_accessed=4_000_000, transcendentals=0),
        name="local_slots",
    )(neighbors, levels, off_blocks, inverse, *payloads)

    pivot, factor = pl.pallas_call(
        functools.partial(second_kernel, capacity, rows),
        out_shape=[
            jax.ShapeDtypeStruct((rows, size, size), bf16),
            jax.ShapeDtypeStruct((rows, slots, size, size), bf16),
        ],
        in_specs=[smem, smem, hbm, hbm, hbm] + [vmem] * (REMOTE + 2),
        out_specs=[vmem, hbm],
        scratch_shapes=[
            pltpu.VMEM((capacity, size, size), bf16),
            pltpu.VMEM((capacity, REMOTE, size, size), bf16),
            pltpu.VMEM((capacity, REMOTE, size, size), bf16),
            pltpu.SemaphoreType.DMA((3,)),
        ],
        input_output_aliases={4: 1},
        compiler_params=params,
        name="second_inverses",
    )(neighbors, levels, diag_blocks, off_blocks, factor, inverse, *received, schur)
    return (pivot, factor)


def solution(mesh):
    in_specs = (
        P(("row", "col"), None, None),
        P(("row", "col"), None, None, None),
        P(("row", "col"), None),
        P(("row", "col")),
    )
    out_specs = (P(("row", "col"), None, None), P(("row", "col"), None, None, None))
    return jax.shard_map(shards, mesh=mesh, in_specs=in_specs, out_specs=out_specs, check_vma=False)
```

```python
import functools
import jax
import jax.numpy as jnp
from jax import lax
from jax.experimental import pallas as pl
from jax.experimental.pallas import tpu as pltpu
from jax.sharding import PartitionSpec as P

NS_STEPS = 4
MIRROR = (1, 0, 3, 2, 5, 4)
VMEM_LIMIT = 40 * 1024 * 1024
REMOTE = 4


def dot(a, b):
    return jnp.dot(a, b, preferred_element_type=jnp.float32)


def dot_t(a, b):
    return lax.dot_general(a, b, (((1,), (1,)), ((), ())), preferred_element_type=jnp.float32)


def halves(value):
    high = value.astype(jnp.bfloat16)
    low = (value - high.astype(jnp.float32)).astype(jnp.bfloat16)
    return high, low


def approx_inverses(matrices, exact):
    size = matrices[0].shape[0]
    eye = (
        lax.broadcasted_iota(jnp.int32, (size, size), 0)
        == lax.broadcasted_iota(jnp.int32, (size, size), 1)
    ).astype(jnp.float32)
    iterates, residuals = [], []
    for matrix in matrices:
        turned = matrix.T
        column = jnp.max(jnp.sum(jnp.abs(matrix), axis=0, keepdims=True), axis=1, keepdims=True)
        row = jnp.max(jnp.sum(jnp.abs(turned), axis=0, keepdims=True), axis=1, keepdims=True)
        scale = 1.0 / (column * row)
        if exact:
            square = dot_t(matrix.astype(jnp.bfloat16), matrix.astype(jnp.bfloat16))
        else:
            high, low = halves(matrix)
            left = jnp.concatenate([high, low], axis=1)
            right = jnp.concatenate(
                [
                    jnp.concatenate([high, high], axis=1),
                    jnp.concatenate([low, low], axis=1),
                ],
                axis=0,
            )
            both = dot_t(left, right)
            square = both[:, :size] + both[:, size:]
        iterates.append(turned * scale)
        residuals.append(eye - square * scale)
    for step in range(NS_STEPS):
        last = step == NS_STEPS - 1
        for n in range(len(matrices)):
            r_high, r_low = halves(residuals[n])
            x_high, x_low = halves(iterates[n])
            row = jnp.concatenate([r_high, r_low], axis=1)
            right = jnp.concatenate([row, row], axis=0)
            left = jnp.concatenate([x_high, x_low], axis=1)
            if not last:
                left = jnp.concatenate([left, row], axis=0)
            both = dot(left, right)
            both = both[:, :size] + both[:, size:]
            iterates[n] = iterates[n] + both[:size]
            if not last:
                residuals[n] = both[size:]
    return iterates


def slot_order():
    row = lax.axis_index("row") % 2
    across = 1 - row
    return (row, 2 + row, across, 3 - row), (row, 3 - row, across, 2 + row)


def transfers(rows, cols):
    steps = [[], [], [], []]
    for r in range(rows):
        for c in range(cols):
            here = r * cols + c
            up, down = (1, 3) if r % 2 == 0 else (3, 1)
            if c + 1 < cols:
                steps[up].append((here, here + 1))
            if c > 0:
                steps[down].append((here, here - 1))
            if r + 1 < rows:
                pair = [(here, here + cols), (here + cols, here)]
                steps[0 if r % 2 == 0 else 2].extend(pair)
    return steps


def masked(block, named):
    return jnp.where(named >= 0, block, jnp.zeros_like(block))


def first_kernel(capacity, diag_hbm, off_hbm, *rest):
    payloads, (inverse, diag, off, sems) = rest[:REMOTE], rest[REMOTE:]
    slots, _ = slot_order()
    copy_diag = pltpu.make_async_copy(diag_hbm, diag, sems.at[0])
    copy_off = pltpu.make_async_copy(off_hbm, off, sems.at[1])
    copy_diag.start()
    copy_off.start()
    copy_diag.wait()
    inverses = approx_inverses([diag[n].astype(jnp.float32) for n in range(capacity)], True)
    inverses = [value.astype(jnp.bfloat16) for value in inverses]
    copy_off.wait()
    for n in range(capacity):
        inverse[n] = inverses[n]
        for j in range(0, REMOTE, 2):
            scaled = dot(inverses[n], jnp.concatenate([off[n, slots[j]], off[n, slots[j + 1]]], axis=1))
            for i in range(2):
                payloads[j + i][n] = inverses[n]
                payloads[j + i][capacity + n] = scaled[:, i * 128 : (i + 1) * 128].astype(jnp.bfloat16)


def local_kernel(
    capacity, rows, neighbors, levels, diag, off, inverse, p0, p1, p2, p3,
    factor_hbm, base, lower, scaled, nothing, sems,
):
    payloads = (p0, p1, p2, p3)
    slots, _ = slot_order()
    start = rows - capacity
    nothing[...] = jnp.zeros_like(nothing)

    def each_remote(act):
        for n in range(capacity):

            @pl.when(levels[n] == 0)
            def _():
                for j in range(REMOTE):
                    target = factor_hbm.at[n, slots[j]]

                    @pl.when(neighbors[n, slots[j]] >= 0)
                    def _():
                        act(pltpu.make_async_copy(payloads[j].at[capacity + n], target, sems.at[0]))

                    @pl.when(neighbors[n, slots[j]] < 0)
                    def _():
                        act(pltpu.make_async_copy(nothing, target, sems.at[0]))

    each_remote(lambda c: c.start())
    for n in range(capacity):
        both = dot(inverse[n], jnp.concatenate([off[n, REMOTE], off[n, REMOTE + 1]], axis=1))
        for i in range(2):
            part = both[:, i * 128 : (i + 1) * 128]
            scaled[n, i] = masked(part, neighbors[n, REMOTE + i]).astype(jnp.bfloat16)

    def local_row(t, carry):
        q = start + t
        total = diag[q].astype(jnp.float32)
        for i in range(2):
            named = neighbors[q, REMOTE + i]
            place = jnp.clip(named % rows, 0, capacity - 1)
            block = masked(off[q, REMOTE + i], named)
            both = dot(block, jnp.concatenate([inverse[place], scaled[place, 1 - i]], axis=1))
            lower[t, i] = both[:, :128].astype(jnp.bfloat16)
            total = total - both[:, 128:]
        base[t] = total
        return carry

    lax.fori_loop(0, capacity, local_row, 0)

    def each_local(act):
        for n in range(rows):
            target = factor_hbm.at[n, pl.ds(REMOTE, 2)]
            if n < capacity:

                @pl.when(levels[n] == 0)
                def _():
                    act(pltpu.make_async_copy(scaled.at[n], target, sems.at[1]))

            if n >= start:

                @pl.when(levels[n] == 1)
                def _():
                    act(pltpu.make_async_copy(lower.at[n - start], target, sems.at[1]))

    each_local(lambda c: c.start())
    each_remote(lambda c: c.wait())
    each_local(lambda c: c.wait())


def take(capacity, rows, t, arrived, neighbors, off, received, lower, total):
    _, slots = slot_order()
    q = rows - capacity + t
    for i, j in enumerate(arrived):
        named = neighbors[q, slots[j]]
        place = jnp.clip(named % rows, 0, capacity - 1)
        block = masked(off[q, slots[j]], named)
        both = dot(block, jnp.concatenate([received[i][place], received[i][capacity + place]], axis=1))
        lower[t, i] = both[:, :128].astype(jnp.bfloat16)
        total = total - both[:, 128:]
    return total


def early_kernel(capacity, rows, arrived, neighbors, off, base, ra, rb, total, lower):
    for t in range(capacity):
        total[t] = take(capacity, rows, t, arrived, neighbors, off, (ra, rb), lower, base[t])


def second_kernel(
    capacity, rows, before, arrived, neighbors, levels, factor_in, off, inverse, total, lower_before, ra, rb,
    pivot, factor_hbm, lower, sems,
):
    del factor_in
    _, slots = slot_order()
    start = rows - capacity

    def each_lower(source, which, sem, act):
        for t in range(capacity):

            @pl.when(levels[start + t] == 1)
            def _():
                for i, j in enumerate(which):
                    act(pltpu.make_async_copy(source.at[t, i], factor_hbm.at[start + t, slots[j]], sem))

    each_lower(lower_before, before, sems.at[0], lambda c: c.start())
    pivots = [
        take(capacity, rows, t, arrived, neighbors, off, (ra, rb), lower, total[t]) for t in range(capacity)
    ]
    each_lower(lower, arrived, sems.at[1], lambda c: c.start())
    inverses = approx_inverses(pivots, False)
    for n in range(rows):
        if n < start:
            pivot[n] = inverse[n]
        elif n >= capacity:
            pivot[n] = inverses[n - start].astype(jnp.bfloat16)
        else:
            pivot[n] = jnp.where(levels[n] == 0, inverse[n], inverses[n - start].astype(jnp.bfloat16))
    each_lower(lower_before, before, sems.at[0], lambda c: c.wait())
    each_lower(lower, arrived, sems.at[1], lambda c: c.wait())


def shards(diag_blocks, off_blocks, neighbors, levels):
    rows, slots = off_blocks.shape[:2]
    size = diag_blocks.shape[1]
    capacity = 3 * rows // 4
    smem = pl.BlockSpec(memory_space=pltpu.SMEM)
    vmem = pl.BlockSpec(memory_space=pltpu.VMEM)
    hbm = pl.BlockSpec(memory_space=pltpu.HBM)
    params = pltpu.CompilerParams(vmem_limit_bytes=VMEM_LIMIT)
    bf16 = jnp.bfloat16
    payload = jax.ShapeDtypeStruct((2 * capacity, size, size), bf16)
    totals = jax.ShapeDtypeStruct((capacity, size, size), jnp.float32)
    factors = jax.ShapeDtypeStruct(off_blocks.shape, bf16)

    diag_blocks = pltpu.with_memory_space_constraint(diag_blocks, pltpu.HBM)
    off_blocks = pltpu.with_memory_space_constraint(off_blocks, pltpu.HBM)
    *payloads, inverse, diag, off = pl.pallas_call(
        functools.partial(first_kernel, capacity),
        out_shape=[payload] * REMOTE
        + [
            jax.ShapeDtypeStruct((capacity, size, size), bf16),
            jax.ShapeDtypeStruct((rows, size, size), bf16),
            factors,
        ],
        in_specs=[hbm, hbm],
        out_specs=[vmem] * (REMOTE + 3),
        scratch_shapes=[pltpu.SemaphoreType.DMA((2,))],
        compiler_params=params,
        name="first_inverses",
    )(diag_blocks, off_blocks)

    steps = transfers(lax.axis_size("row"), lax.axis_size("col"))
    received = [lax.ppermute(payloads[j], ("row", "col"), steps[j]) for j in range(REMOTE)]

    factor, base = pl.pallas_call(
        functools.partial(local_kernel, capacity, rows),
        out_shape=[factors, totals],
        in_specs=[smem, smem] + [vmem] * (REMOTE + 3),
        out_specs=[hbm, vmem],
        scratch_shapes=[
            pltpu.VMEM((capacity, 2, size, size), bf16),
            pltpu.VMEM((capacity, 2, size, size), bf16),
            pltpu.VMEM((size, size), bf16),
            pltpu.SemaphoreType.DMA((2,)),
        ],
        compiler_params=params,
        cost_estimate=pl.CostEstimate(flops=400_000_000, bytes_accessed=4_000_000, transcendentals=0),
        name="local_slots",
    )(neighbors, levels, diag, off, inverse, *payloads)

    before, after = (0, 1), (2, 3)
    total, lower = pl.pallas_call(
        functools.partial(early_kernel, capacity, rows, before),
        out_shape=[totals, jax.ShapeDtypeStruct((capacity, 2, size, size), bf16)],
        in_specs=[smem] + [vmem] * 4,
        out_specs=[vmem, vmem],
        compiler_params=params,
        name="early_slots",
    )(neighbors, off, base, *(received[j] for j in before))

    pivot, factor = pl.pallas_call(
        functools.partial(second_kernel, capacity, rows, before, after),
        out_shape=[jax.ShapeDtypeStruct((rows, size, size), bf16), factors],
        in_specs=[smem, smem, hbm] + [vmem] * 6,
        out_specs=[vmem, hbm],
        scratch_shapes=[
            pltpu.VMEM((capacity, 2, size, size), bf16),
            pltpu.SemaphoreType.DMA((2,)),
        ],
        input_output_aliases={2: 1},
        compiler_params=params,
        name="second_inverses",
    )(neighbors, levels, factor, off, inverse, total, lower, *(received[j] for j in after))
    return (pivot, factor)


def solution(mesh):
    in_specs = (
        P(("row", "col"), None, None),
        P(("row", "col"), None, None, None),
        P(("row", "col"), None),
        P(("row", "col")),
    )
    out_specs = (P(("row", "col"), None, None), P(("row", "col"), None, None, None))
    return jax.shard_map(shards, mesh=mesh, in_specs=in_specs, out_specs=out_specs, check_vma=False)
```

```python
import functools
import jax
import jax.numpy as jnp
from jax import lax
from jax.experimental import pallas as pl
from jax.experimental.pallas import tpu as pltpu
from jax.sharding import PartitionSpec as P

NS_STEPS = 4
MIRROR = (1, 0, 3, 2, 5, 4)
VMEM_LIMIT = 40 * 1024 * 1024
REMOTE = 4
ROW_PAIRS = (3, 0, 3, 1, 3, 0, 3, 2)
COL_PAIRS = ((1, 0), (2, 1), (1, 2), (2, 0), (2, 0), (1, 2), (2, 1), (1, 0))


def dot(a, b):
    return jnp.dot(a, b, preferred_element_type=jnp.float32)


def dot_t(a, b):
    return lax.dot_general(a, b, (((1,), (1,)), ((), ())), preferred_element_type=jnp.float32)


def halves(value):
    high = value.astype(jnp.bfloat16)
    low = (value - high.astype(jnp.float32)).astype(jnp.bfloat16)
    return high, low


def approx_inverses(matrices, exact):
    size = matrices[0].shape[0]
    eye = (
        lax.broadcasted_iota(jnp.int32, (size, size), 0)
        == lax.broadcasted_iota(jnp.int32, (size, size), 1)
    ).astype(jnp.float32)
    iterates, residuals = [], []
    for matrix in matrices:
        turned = matrix.T
        column = jnp.max(jnp.sum(jnp.abs(matrix), axis=0, keepdims=True), axis=1, keepdims=True)
        row = jnp.max(jnp.sum(jnp.abs(turned), axis=0, keepdims=True), axis=1, keepdims=True)
        scale = 1.0 / (column * row)
        if exact:
            square = dot_t(matrix.astype(jnp.bfloat16), matrix.astype(jnp.bfloat16))
        else:
            high, low = halves(matrix)
            left = jnp.concatenate([high, low], axis=1)
            right = jnp.concatenate(
                [
                    jnp.concatenate([high, high], axis=1),
                    jnp.concatenate([low, low], axis=1),
                ],
                axis=0,
            )
            both = dot_t(left, right)
            square = both[:, :size] + both[:, size:]
        iterates.append(turned * scale)
        residuals.append(eye - square * scale)
    for step in range(NS_STEPS):
        last = step == NS_STEPS - 1
        for n in range(len(matrices)):
            r_high, r_low = halves(residuals[n])
            x_high, x_low = halves(iterates[n])
            row = jnp.concatenate([r_high, r_low], axis=1)
            right = jnp.concatenate([row, row], axis=0)
            left = jnp.concatenate([x_high, x_low], axis=1)
            if not last:
                left = jnp.concatenate([left, row], axis=0)
            both = dot(left, right)
            both = both[:, :size] + both[:, size:]
            iterates[n] = iterates[n] + both[:size]
            if not last:
                residuals[n] = both[size:]
    return iterates


def row_colour(r):
    return ROW_PAIRS[r % len(ROW_PAIRS)]


def col_colour(r, c):
    return COL_PAIRS[r % len(COL_PAIRS)][1 - c % 2]


def transfers(rows, cols):
    steps = [[] for _ in range(REMOTE)]
    for r in range(rows):
        for c in range(cols):
            here = r * cols + c
            if r + 1 < rows:
                steps[row_colour(r)] += [(here, here + cols), (here + cols, here)]
            if c + 1 < cols:
                steps[col_colour(r, c)] += [(here, here + 1), (here + 1, here)]
    return steps


def slot_order():
    period = len(ROW_PAIRS)
    row = lax.rem(lax.axis_index("row"), period)
    col = lax.rem(lax.axis_index("col"), 2)
    code = jnp.int32(0)
    for r in range(period):
        packed = 0
        for c in range(2):
            colours = (row_colour(r), row_colour(r + period - 1), col_colour(r, c), col_colour(r, c + 1))
            for slot, j in enumerate(colours):
                packed |= slot << (8 * c + 2 * j)
        code = jnp.where(row == r, jnp.int32(packed), code)
    code = lax.shift_right_logical(code, 8 * col)
    return tuple(lax.shift_right_logical(code, 2 * j) & 3 for j in range(REMOTE))


def masked(block, named):
    return jnp.where(named >= 0, block, jnp.zeros_like(block))


def first_kernel(capacity, diag_hbm, off_hbm, *rest):
    payloads, (inverse, diag, off, sems) = rest[:REMOTE], rest[REMOTE:]
    copies = [pltpu.make_async_copy(diag_hbm, diag, sems.at[0])]
    for j, slot in enumerate(slot_order()):
        source = off_hbm.at[pl.ds(0, capacity), slot]
        copies.append(pltpu.make_async_copy(source, payloads[j].at[pl.ds(capacity, capacity)], sems.at[1 + j]))
    copies.append(pltpu.make_async_copy(off_hbm, off, sems.at[1 + REMOTE]))
    for copy in copies:
        copy.start()
    copies[0].wait()
    inverses = approx_inverses([diag[n].astype(jnp.float32) for n in range(capacity)], True)
    for n in range(capacity):
        value = inverses[n].astype(jnp.bfloat16)
        inverse[n] = value
        for payload in payloads:
            payload[n] = value
    for copy in copies[1:]:
        copy.wait()


def pair_sums(blocks, inverses, uppers):
    lowers = [dot(block, inverse).astype(jnp.bfloat16) for block, inverse in zip(blocks, inverses)]
    return lowers, dot(jnp.concatenate(lowers, axis=1), jnp.concatenate(uppers, axis=0))


def local_kernel(
    capacity, rows, neighbors, levels, diag, off, inverse, factor_hbm, base, lower, scaled, sems,
):
    start = rows - capacity
    slots = off.shape[1]
    for n in range(capacity):
        for k in range(0, slots, 2):
            both = dot(inverse[n], jnp.concatenate([off[n, k], off[n, k + 1]], axis=1))
            for i in range(2):
                part = both[:, i * 128 : (i + 1) * 128]
                scaled[n, k + i] = masked(part, neighbors[n, k + i]).astype(jnp.bfloat16)

    def local_row(t, carry):
        q = start + t
        blocks, inverses, uppers = [], [], []
        for i in range(2):
            named = neighbors[q, REMOTE + i]
            place = jnp.clip(lax.rem(named, rows), 0, capacity - 1)
            blocks.append(masked(off[q, REMOTE + i], named))
            inverses.append(inverse[place])
            uppers.append(off[place, REMOTE + 1 - i])
        lowers, total = pair_sums(blocks, inverses, uppers)
        for i in range(2):
            lower[t, i] = lowers[i]
        base[t] = diag[q].astype(jnp.float32) - total
        return carry

    lax.fori_loop(0, capacity, local_row, 0)

    def each(act):
        for n in range(rows):
            if n < capacity:

                @pl.when(levels[n] == 0)
                def _():
                    act(pltpu.make_async_copy(scaled.at[n], factor_hbm.at[n], sems.at[0]))

            if n >= start:

                @pl.when(levels[n] == 1)
                def _():
                    target = factor_hbm.at[n, pl.ds(REMOTE, 2)]
                    act(pltpu.make_async_copy(lower.at[n - start], target, sems.at[1]))

    each(lambda c: c.start())
    each(lambda c: c.wait())


def take(capacity, rows, t, arrived, neighbors, off, received, lower, total):
    slots = slot_order()
    q = rows - capacity + t
    blocks, inverses, uppers = [], [], []
    for i, j in enumerate(arrived):
        named = neighbors[q, slots[j]]
        place = jnp.clip(lax.rem(named, rows), 0, capacity - 1)
        blocks.append(masked(off[q, slots[j]], named))
        inverses.append(received[i][place])
        uppers.append(received[i][capacity + place])
    lowers, gained = pair_sums(blocks, inverses, uppers)
    for i in range(len(arrived)):
        lower[t, i] = lowers[i]
    return total - gained


def early_kernel(capacity, rows, arrived, neighbors, off, base, ra, rb, total, lower):
    for t in range(capacity):
        total[t] = take(capacity, rows, t, arrived, neighbors, off, (ra, rb), lower, base[t])


def second_kernel(
    capacity, rows, before, arrived, neighbors, levels, factor_in, off, inverse, total, lower_before, ra, rb,
    pivot, factor_hbm, lower, sems,
):
    del factor_in
    slots = slot_order()
    start = rows - capacity

    def each_lower(source, which, sem, act):
        for t in range(capacity):

            @pl.when(levels[start + t] == 1)
            def _():
                for i, j in enumerate(which):
                    act(pltpu.make_async_copy(source.at[t, i], factor_hbm.at[start + t, slots[j]], sem))

    each_lower(lower_before, before, sems.at[0], lambda c: c.start())
    pivots = [
        take(capacity, rows, t, arrived, neighbors, off, (ra, rb), lower, total[t]) for t in range(capacity)
    ]
    each_lower(lower, arrived, sems.at[1], lambda c: c.start())
    inverses = approx_inverses(pivots, False)
    for n in range(rows):
        if n < start:
            pivot[n] = inverse[n]
        elif n >= capacity:
            pivot[n] = inverses[n - start].astype(jnp.bfloat16)
        else:
            pivot[n] = jnp.where(levels[n] == 0, inverse[n], inverses[n - start].astype(jnp.bfloat16))
    each_lower(lower_before, before, sems.at[0], lambda c: c.wait())
    each_lower(lower, arrived, sems.at[1], lambda c: c.wait())


def shards(diag_blocks, off_blocks, neighbors, levels):
    rows, slots = off_blocks.shape[:2]
    size = diag_blocks.shape[1]
    capacity = 3 * rows // 4
    smem = pl.BlockSpec(memory_space=pltpu.SMEM)
    vmem = pl.BlockSpec(memory_space=pltpu.VMEM)
    hbm = pl.BlockSpec(memory_space=pltpu.HBM)
    params = pltpu.CompilerParams(vmem_limit_bytes=VMEM_LIMIT)
    bf16 = jnp.bfloat16
    payload = jax.ShapeDtypeStruct((2 * capacity, size, size), bf16)
    totals = jax.ShapeDtypeStruct((capacity, size, size), jnp.float32)
    factors = jax.ShapeDtypeStruct(off_blocks.shape, bf16)

    diag_blocks = pltpu.with_memory_space_constraint(diag_blocks, pltpu.HBM)
    off_blocks = pltpu.with_memory_space_constraint(off_blocks, pltpu.HBM)
    *payloads, inverse, diag, off = pl.pallas_call(
        functools.partial(first_kernel, capacity),
        out_shape=[payload] * REMOTE
        + [
            jax.ShapeDtypeStruct((capacity, size, size), bf16),
            jax.ShapeDtypeStruct((rows, size, size), bf16),
            factors,
        ],
        in_specs=[hbm, hbm],
        out_specs=[vmem] * (REMOTE + 3),
        scratch_shapes=[pltpu.SemaphoreType.DMA((REMOTE + 2,))],
        compiler_params=params,
        name="first_inverses",
    )(diag_blocks, off_blocks)

    steps = transfers(lax.axis_size("row"), lax.axis_size("col"))
    received = [lax.ppermute(payloads[j], ("row", "col"), steps[j]) for j in range(REMOTE)]

    factor, base = pl.pallas_call(
        functools.partial(local_kernel, capacity, rows),
        out_shape=[factors, totals],
        in_specs=[smem, smem] + [vmem] * 3,
        out_specs=[hbm, vmem],
        scratch_shapes=[
            pltpu.VMEM((capacity, 2, size, size), bf16),
            pltpu.VMEM((capacity, slots, size, size), bf16),
            pltpu.SemaphoreType.DMA((2,)),
        ],
        compiler_params=params,
        cost_estimate=pl.CostEstimate(flops=400_000_000, bytes_accessed=4_000_000, transcendentals=0),
        name="local_slots",
    )(neighbors, levels, diag, off, inverse)

    before, after = (0, 1), (2, 3)
    total, lower = pl.pallas_call(
        functools.partial(early_kernel, capacity, rows, before),
        out_shape=[totals, jax.ShapeDtypeStruct((capacity, 2, size, size), bf16)],
        in_specs=[smem] + [vmem] * 4,
        out_specs=[vmem, vmem],
        compiler_params=params,
        name="early_slots",
    )(neighbors, off, base, *(received[j] for j in before))

    pivot, factor = pl.pallas_call(
        functools.partial(second_kernel, capacity, rows, before, after),
        out_shape=[jax.ShapeDtypeStruct((rows, size, size), bf16), factors],
        in_specs=[smem, smem, hbm] + [vmem] * 6,
        out_specs=[vmem, hbm],
        scratch_shapes=[
            pltpu.VMEM((capacity, 2, size, size), bf16),
            pltpu.SemaphoreType.DMA((2,)),
        ],
        input_output_aliases={2: 1},
        compiler_params=params,
        name="second_inverses",
    )(neighbors, levels, factor, off, inverse, total, lower, *(received[j] for j in after))
    return (pivot, factor)


def solution(mesh):
    in_specs = (
        P(("row", "col"), None, None),
        P(("row", "col"), None, None, None),
        P(("row", "col"), None),
        P(("row", "col")),
    )
    out_specs = (P(("row", "col"), None, None), P(("row", "col"), None, None, None))
    return jax.shard_map(shards, mesh=mesh, in_specs=in_specs, out_specs=out_specs, check_vma=False)
```

```python
import functools
import jax
import jax.numpy as jnp
from jax import lax
from jax.experimental import pallas as pl
from jax.experimental.pallas import tpu as pltpu
from jax.sharding import PartitionSpec as P

NS_STEPS = 4
MIRROR = (1, 0, 3, 2, 5, 4)
VMEM_LIMIT = 40 * 1024 * 1024
REMOTE = 4
ROW_PAIRS = (3, 0, 3, 1)
COL_PAIRS = ((2, 0), (1, 2), (1, 2), (2, 0))


def dot(a, b):
    return jnp.dot(a, b, preferred_element_type=jnp.float32)


def dot_t(a, b):
    return lax.dot_general(a, b, (((1,), (1,)), ((), ())), preferred_element_type=jnp.float32)


def halves(value):
    high = value.astype(jnp.bfloat16)
    low = (value - high.astype(jnp.float32)).astype(jnp.bfloat16)
    return high, low


def approx_inverses(matrices, exact):
    size = matrices[0].shape[0]
    eye = (
        lax.broadcasted_iota(jnp.int32, (size, size), 0)
        == lax.broadcasted_iota(jnp.int32, (size, size), 1)
    ).astype(jnp.float32)
    iterates, residuals = [], []
    for matrix in matrices:
        turned = matrix.T
        column = jnp.max(jnp.sum(jnp.abs(matrix), axis=0, keepdims=True), axis=1, keepdims=True)
        row = jnp.max(jnp.sum(jnp.abs(turned), axis=0, keepdims=True), axis=1, keepdims=True)
        scale = 1.0 / (column * row)
        if exact:
            square = dot_t(matrix.astype(jnp.bfloat16), matrix.astype(jnp.bfloat16))
        else:
            high, low = halves(matrix)
            left = jnp.concatenate([high, low], axis=1)
            right = jnp.concatenate(
                [
                    jnp.concatenate([high, high], axis=1),
                    jnp.concatenate([low, low], axis=1),
                ],
                axis=0,
            )
            both = dot_t(left, right)
            square = both[:, :size] + both[:, size:]
        iterates.append(turned * scale)
        residuals.append(eye - square * scale)
    for step in range(NS_STEPS):
        last = step == NS_STEPS - 1
        for n in range(len(matrices)):
            r_high, r_low = halves(residuals[n])
            x_high, x_low = halves(iterates[n])
            row = jnp.concatenate([r_high, r_low], axis=1)
            right = jnp.concatenate([row, row], axis=0)
            left = jnp.concatenate([x_high, x_low], axis=1)
            if not last:
                left = jnp.concatenate([row, left], axis=0)
            both = dot(left, right)
            both = both[:, :size] + both[:, size:]
            iterates[n] = iterates[n] + both[-size:]
            if not last:
                residuals[n] = both[:size]
    return iterates


def row_colour(r):
    return ROW_PAIRS[r % len(ROW_PAIRS)]


def col_colour(r, c):
    return COL_PAIRS[r % len(COL_PAIRS)][1 - c % 2]


def transfers(rows, cols):
    steps = [[] for _ in range(REMOTE)]
    for r in range(rows):
        for c in range(cols):
            here = r * cols + c
            if r + 1 < rows:
                steps[row_colour(r)] += [(here, here + cols), (here + cols, here)]
            if c + 1 < cols:
                steps[col_colour(r, c)] += [(here, here + 1), (here + 1, here)]
    return steps


def slot_order():
    period = len(ROW_PAIRS)
    row = lax.rem(lax.axis_index("row"), period)
    col = lax.rem(lax.axis_index("col"), 2)
    code = jnp.int32(0)
    for r in range(period):
        packed = 0
        for c in range(2):
            colours = (row_colour(r), row_colour(r + period - 1), col_colour(r, c), col_colour(r, c + 1))
            for slot, j in enumerate(colours):
                packed |= slot << (8 * c + 2 * j)
        code = jnp.where(row == r, jnp.int32(packed), code)
    code = lax.shift_right_logical(code, 8 * col)
    return tuple(lax.shift_right_logical(code, 2 * j) & 3 for j in range(REMOTE))


def masked(block, named):
    return jnp.where(named >= 0, block, jnp.zeros_like(block))


def first_kernel(
    capacity, rows, neighbors_hbm, levels_hbm, diag_hbm, off_hbm, p0, p1, p2, p3, inverse, diag, off,
    neighbors, levels, places, sems,
):
    payloads = (p0, p1, p2, p3)
    slots = slot_order()
    start = rows - capacity
    copies = [
        pltpu.make_async_copy(neighbors_hbm, neighbors, sems.at[0]),
        pltpu.make_async_copy(levels_hbm, levels, sems.at[1]),
        pltpu.make_async_copy(diag_hbm, diag, sems.at[2]),
        pltpu.make_async_copy(off_hbm, off, sems.at[3]),
    ]
    for copy in copies:
        copy.start()
    copies[0].wait()
    copies[1].wait()
    for j in range(REMOTE):
        for t in range(capacity):
            places[j * rows + t] = 0
        for n in range(capacity):
            named = neighbors[n, slots[j]]
            live = jnp.logical_and(named >= 0, levels[n] == 0)
            places[j * rows + jnp.where(live, lax.rem(named, rows) - start, capacity)] = n
    for j in range(REMOTE):
        for t in range(capacity):
            pltpu.make_async_copy(
                off_hbm.at[places[j * rows + t], slots[j]], payloads[j].at[capacity + t], sems.at[4 + j]
            ).start()
    copies[2].wait()
    inverses = approx_inverses([diag[n].astype(jnp.float32) for n in range(capacity)], True)
    for n in range(capacity):
        inverse[n] = inverses[n].astype(jnp.bfloat16)

    def pack(t, carry):
        for j in range(REMOTE):
            payloads[j][t] = inverse[places[j * rows + t]]
        return carry

    lax.fori_loop(0, capacity, pack, 0)
    copies[3].wait()
    for j in range(REMOTE):
        whole = payloads[j].at[pl.ds(capacity, capacity)]
        pltpu.make_async_copy(off_hbm.at[pl.ds(0, capacity), 0], whole, sems.at[4 + j]).wait()


def pair_sums(blocks, inverses, uppers):
    lowers = [dot(block, inverse).astype(jnp.bfloat16) for block, inverse in zip(blocks, inverses)]
    return lowers, dot(jnp.concatenate(lowers, axis=1), jnp.concatenate(uppers, axis=0))


def local_kernel(
    capacity, rows, neighbors, levels, diag, off, inverse, factor_hbm, base, remote, kept, late, lower, scaled, sems,
):
    start = rows - capacity
    slots = off.shape[1]
    order = slot_order()
    for n in range(capacity):
        for k in range(0, slots, 2):
            both = dot(inverse[n], jnp.concatenate([off[n, k], off[n, k + 1]], axis=1))
            for i in range(2):
                part = masked(both[:, i * 128 : (i + 1) * 128], neighbors[n, k + i]).astype(jnp.bfloat16)
                scaled[n, k + i] = part
                if n >= start and k < REMOTE:
                    kept[n - start, k + i] = part

    def local_row(t, carry):
        q = start + t
        blocks, inverses, uppers = [], [], []
        for i in range(2):
            named = neighbors[q, REMOTE + i]
            place = jnp.clip(lax.rem(named, rows), 0, capacity - 1)
            blocks.append(masked(off[q, REMOTE + i], named))
            inverses.append(inverse[place])
            uppers.append(off[place, REMOTE + 1 - i])
        lowers, total = pair_sums(blocks, inverses, uppers)
        for i in range(2):
            lower[t, i] = lowers[i]
        base[t] = diag[q].astype(jnp.float32) - total
        for j in range(REMOTE):
            live = jnp.where(levels[q] == 1, neighbors[q, order[j]], -1)
            remote[j, t] = masked(off[q, order[j]], live)
        late[t] = jnp.full(late.shape[1:], levels[q].astype(jnp.float32))
        return carry

    lax.fori_loop(0, capacity, local_row, 0)

    def each(act):
        for n in range(rows):
            if n < start:
                act(pltpu.make_async_copy(scaled.at[n], factor_hbm.at[n], sems.at[0]))
                continue
            target = factor_hbm.at[n, pl.ds(REMOTE, 2)]

            @pl.when(levels[n] == 1)
            def _():
                act(pltpu.make_async_copy(lower.at[n - start], target, sems.at[1]))

            if n < capacity:

                @pl.when(levels[n] == 0)
                def _():
                    act(pltpu.make_async_copy(scaled.at[n, pl.ds(REMOTE, 2)], target, sems.at[1]))

    each(lambda c: c.start())
    each(lambda c: c.wait())


def take(capacity, t, arrived, remote, received, late, kept, total):
    order = slot_order()
    lowers, gained = pair_sums(
        [remote[j, t] for j in arrived],
        [blocks[t] for blocks in received],
        [blocks[capacity + t] for blocks in received],
    )
    is_late = late[t][:1] > 0.5
    for j, lower in zip(arrived, lowers):
        kept[t, order[j]] = jnp.where(is_late, lower, kept[t, order[j]])
    return total - gained


def early_kernel(capacity, arrived, remote, base, late, kept_in, ra, rb, total, kept):
    del kept_in
    for t in range(capacity):
        total[t] = take(capacity, t, arrived, remote, (ra, rb), late, kept, base[t])


def second_kernel(
    capacity, rows, arrived, factor_in, kept_in, inverse, total, remote, late, ra, rb, pivot, factor_hbm, kept, sem,
):
    del factor_in, kept_in
    start = rows - capacity
    pivots = [take(capacity, t, arrived, remote, (ra, rb), late, kept, total[t]) for t in range(capacity)]
    copy = pltpu.make_async_copy(kept, factor_hbm.at[pl.ds(start, capacity), pl.ds(0, REMOTE)], sem)
    copy.start()
    inverses = approx_inverses(pivots, False)
    for n in range(rows):
        if n < start:
            pivot[n] = inverse[n]
            continue
        value = inverses[n - start].astype(jnp.bfloat16)
        if n < capacity:
            value = jnp.where(late[n - start][:1] > 0.5, value, inverse[n])
        pivot[n] = value
    copy.wait()


def shards(diag_blocks, off_blocks, neighbors, levels):
    rows, slots = off_blocks.shape[:2]
    size = diag_blocks.shape[1]
    capacity = 3 * rows // 4
    smem = pl.BlockSpec(memory_space=pltpu.SMEM)
    vmem = pl.BlockSpec(memory_space=pltpu.VMEM)
    hbm = pl.BlockSpec(memory_space=pltpu.HBM)
    params = pltpu.CompilerParams(vmem_limit_bytes=VMEM_LIMIT)
    bf16 = jnp.bfloat16
    payload = jax.ShapeDtypeStruct((2 * capacity, size, size), bf16)
    totals = jax.ShapeDtypeStruct((capacity, size, size), jnp.float32)
    factors = jax.ShapeDtypeStruct(off_blocks.shape, bf16)
    pivots = jax.ShapeDtypeStruct((rows, size, size), bf16)
    kepts = jax.ShapeDtypeStruct((capacity, REMOTE, size, size), bf16)

    diag_blocks, off_blocks, neighbors, levels = (
        pltpu.with_memory_space_constraint(value, pltpu.HBM)
        for value in (diag_blocks, off_blocks, neighbors, levels)
    )
    *payloads, inverse, diag, off = pl.pallas_call(
        functools.partial(first_kernel, capacity, rows),
        out_shape=[payload] * REMOTE + [jax.ShapeDtypeStruct((capacity, size, size), bf16), pivots, factors],
        in_specs=[hbm] * 4,
        out_specs=[vmem] * (REMOTE + 3),
        scratch_shapes=[
            pltpu.SMEM(neighbors.shape, jnp.int32),
            pltpu.SMEM(levels.shape, jnp.int32),
            pltpu.SMEM((REMOTE * rows,), jnp.int32),
            pltpu.SemaphoreType.DMA((4 + REMOTE,)),
        ],
        compiler_params=params,
        name="first_inverses",
    )(neighbors, levels, diag_blocks, off_blocks)

    steps = transfers(lax.axis_size("row"), lax.axis_size("col"))
    received = [lax.ppermute(payloads[j], ("row", "col"), steps[j]) for j in range(REMOTE)]

    factor, base, remote, kept, late = pl.pallas_call(
        functools.partial(local_kernel, capacity, rows),
        out_shape=[
            factors,
            totals,
            jax.ShapeDtypeStruct((REMOTE, capacity, size, size), bf16),
            kepts,
            jax.ShapeDtypeStruct((capacity, 8, size), jnp.float32),
        ],
        in_specs=[smem, smem] + [vmem] * 3,
        out_specs=[hbm] + [vmem] * 4,
        scratch_shapes=[
            pltpu.VMEM((capacity, 2, size, size), bf16),
            pltpu.VMEM((capacity, slots, size, size), bf16),
            pltpu.SemaphoreType.DMA((2,)),
        ],
        compiler_params=params,
        cost_estimate=pl.CostEstimate(flops=400_000_000, bytes_accessed=4_000_000, transcendentals=0),
        name="local_slots",
    )(neighbors, levels, diag, off, inverse)

    before, after = (0, 1), (2, 3)
    total, kept = pl.pallas_call(
        functools.partial(early_kernel, capacity, before),
        out_shape=[totals, kepts],
        in_specs=[vmem] * 6,
        out_specs=[vmem, vmem],
        input_output_aliases={3: 1},
        compiler_params=params,
        name="early_slots",
    )(remote, base, late, kept, *(received[j] for j in before))

    pivot, factor, _ = pl.pallas_call(
        functools.partial(second_kernel, capacity, rows, after),
        out_shape=[pivots, factors, kepts],
        in_specs=[hbm] + [vmem] * 7,
        out_specs=[vmem, hbm, vmem],
        scratch_shapes=[pltpu.SemaphoreType.DMA],
        input_output_aliases={0: 1, 1: 2},
        compiler_params=params,
        name="second_inverses",
    )(factor, kept, inverse, total, remote, late, *(received[j] for j in after))
    return (pivot, factor)


def solution(mesh):
    in_specs = (
        P(("row", "col"), None, None),
        P(("row", "col"), None, None, None),
        P(("row", "col"), None),
        P(("row", "col")),
    )
    out_specs = (P(("row", "col"), None, None), P(("row", "col"), None, None, None))
    return jax.shard_map(shards, mesh=mesh, in_specs=in_specs, out_specs=out_specs, check_vma=False)
```

```python
import functools
import jax
import jax.numpy as jnp
from jax import lax
from jax.experimental import pallas as pl
from jax.experimental.pallas import tpu as pltpu
from jax.sharding import PartitionSpec as P

NS_STEPS = 4
MIRROR = (1, 0, 3, 2, 5, 4)
VMEM_LIMIT = 40 * 1024 * 1024
REMOTE = 4
EVERY_DEVICE = (
    ((6, 0, 2, 4), (6, 2, 3, 0), (6, 3, 2, 0), (0, 6, 3, 4)),
    ((2, 1, 0, 5), (3, 2, 0, 1), (0, 3, 2, 1), (1, 0, 3, 5)),
    ((2, 0, 1, 4), (3, 2, 1, 0), (1, 3, 0, 2), (0, 1, 4, 3)),
    ((0, 1, 2, 5), (0, 2, 3, 1), (0, 3, 1, 2), (1, 0, 5, 3)),
    ((1, 2, 4, 0), (1, 3, 2, 0), (1, 0, 3, 2), (0, 1, 4, 3)),
    ((0, 2, 5, 1), (0, 3, 2, 1), (0, 1, 3, 2), (1, 0, 5, 3)),
    ((1, 0, 2, 4), (1, 2, 3, 0), (1, 3, 2, 0), (4, 1, 3, 0)),
    ((6, 1, 2, 5), (6, 2, 3, 1), (6, 3, 2, 1), (5, 6, 3, 1)),
)
ANY_MESH = (
    ((2, 1, 3, 0), (3, 1, 2, 0)),
    ((0, 3, 2, 1), (0, 2, 3, 1)),
    ((1, 3, 2, 0), (1, 2, 3, 0)),
    ((2, 0, 3, 1), (3, 0, 2, 1)),
)


def dot(a, b):
    return jnp.dot(a, b, preferred_element_type=jnp.float32)


def dot_t(a, b):
    return lax.dot_general(a, b, (((1,), (1,)), ((), ())), preferred_element_type=jnp.float32)


def halves(value):
    high = value.astype(jnp.bfloat16)
    low = (value - high.astype(jnp.float32)).astype(jnp.bfloat16)
    return high, low


def approx_inverses(matrices, exact):
    size = matrices[0].shape[0]
    eye = (
        lax.broadcasted_iota(jnp.int32, (size, size), 0)
        == lax.broadcasted_iota(jnp.int32, (size, size), 1)
    ).astype(jnp.float32)
    iterates, residuals = [], []
    for matrix in matrices:
        turned = matrix.T
        column = jnp.max(jnp.sum(jnp.abs(matrix), axis=0, keepdims=True), axis=1, keepdims=True)
        row = jnp.max(jnp.sum(jnp.abs(turned), axis=0, keepdims=True), axis=1, keepdims=True)
        scale = 1.0 / (column * row)
        if exact:
            square = dot_t(matrix.astype(jnp.bfloat16), matrix.astype(jnp.bfloat16))
        else:
            high, low = halves(matrix)
            left = jnp.concatenate([high, low], axis=1)
            right = jnp.concatenate(
                [
                    jnp.concatenate([high, high], axis=1),
                    jnp.concatenate([low, low], axis=1),
                ],
                axis=0,
            )
            both = dot_t(left, right)
            square = both[:, :size] + both[:, size:]
        iterates.append(turned * scale)
        residuals.append(eye - square * scale)
    for step in range(NS_STEPS):
        last = step == NS_STEPS - 1
        for n in range(len(matrices)):
            r_high, r_low = halves(residuals[n])
            x_high, x_low = halves(iterates[n])
            row = jnp.concatenate([r_high, r_low], axis=1)
            right = jnp.concatenate([row, row], axis=0)
            left = jnp.concatenate([x_high, x_low], axis=1)
            if not last:
                left = jnp.concatenate([row, left], axis=0)
            both = dot(left, right)
            both = both[:, :size] + both[:, size:]
            iterates[n] = iterates[n] + both[-size:]
            if not last:
                residuals[n] = both[:size]
    return iterates


def meetings(rows, cols):
    return EVERY_DEVICE if (rows, cols) == (8, 4) else ANY_MESH


def transfers(rows, cols):
    plan = meetings(rows, cols)
    steps = [[] for _ in range(REMOTE)]
    for r in range(rows):
        for c in range(cols):
            around = ((r + 1, c), (r - 1, c), (r, c + 1), (r, c - 1), (r + 1, c), (r - 1, c), (rows - 1 - r, c))
            entry = plan[r % len(plan)][c % len(plan[0])]
            for j in range(REMOTE):
                to_row, to_col = around[entry[j]]
                if 0 <= to_row < rows and 0 <= to_col < cols:
                    steps[j].append((r * cols + c, to_row * cols + to_col))
    return steps


def slot_order():
    plan = meetings(lax.axis_size("row"), lax.axis_size("col"))
    row = lax.rem(lax.axis_index("row"), len(plan))
    col = lax.rem(lax.axis_index("col"), len(plan[0]))
    code = jnp.int32(0)
    for r, line in enumerate(plan):
        for c, entry in enumerate(line):
            packed = sum(min(entry[j], REMOTE) << (3 * j) for j in range(REMOTE))
            code = jnp.where(row * len(line) + col == r * len(line) + c, jnp.int32(packed), code)
    return tuple(lax.shift_right_logical(code, 3 * j) & 7 for j in range(REMOTE))


def masked(block, named):
    return jnp.where(named >= 0, block, jnp.zeros_like(block))


def first_kernel(
    capacity, rows, neighbors_hbm, levels_hbm, diag_hbm, off_hbm, p0, p1, p2, p3, inverse, diag, off,
    neighbors, levels, places, sems,
):
    payloads = (p0, p1, p2, p3)
    slots = slot_order()
    start = rows - capacity
    copies = [
        pltpu.make_async_copy(neighbors_hbm, neighbors, sems.at[0]),
        pltpu.make_async_copy(levels_hbm, levels, sems.at[1]),
        pltpu.make_async_copy(diag_hbm, diag, sems.at[2]),
        pltpu.make_async_copy(off_hbm, off, sems.at[3]),
    ]
    for copy in copies:
        copy.start()
    copies[0].wait()
    copies[1].wait()
    for j in range(REMOTE):
        for t in range(capacity):
            places[j * rows + t] = 0
        for n in range(capacity):
            named = neighbors[n, slots[j]]
            live = jnp.logical_and(named >= 0, levels[n] == 0)
            places[j * rows + jnp.where(live, lax.rem(named, rows) - start, capacity)] = n
    for j in range(REMOTE):
        for t in range(capacity):
            pltpu.make_async_copy(
                off_hbm.at[places[j * rows + t], slots[j]], payloads[j].at[capacity + t], sems.at[4 + j]
            ).start()
    copies[2].wait()
    inverses = approx_inverses([diag[n].astype(jnp.float32) for n in range(capacity)], True)
    for n in range(capacity):
        inverse[n] = inverses[n].astype(jnp.bfloat16)

    def pack(t, carry):
        for j in range(REMOTE):
            payloads[j][t] = inverse[places[j * rows + t]]
        return carry

    lax.fori_loop(0, capacity, pack, 0)
    copies[3].wait()
    for j in range(REMOTE):
        whole = payloads[j].at[pl.ds(capacity, capacity)]
        pltpu.make_async_copy(off_hbm.at[pl.ds(0, capacity), 0], whole, sems.at[4 + j]).wait()


def pair_sums(blocks, inverses, uppers):
    lowers = [dot(block, inverse).astype(jnp.bfloat16) for block, inverse in zip(blocks, inverses)]
    return lowers, dot(jnp.concatenate(lowers, axis=1), jnp.concatenate(uppers, axis=0))


def local_kernel(
    capacity, rows, neighbors, levels, diag, off, inverse, factor_hbm, base, remote, kept, late, lower, scaled, sems,
):
    start = rows - capacity
    slots = off.shape[1]
    order = slot_order()
    for n in range(capacity):
        for k in range(0, slots, 2):
            both = dot(inverse[n], jnp.concatenate([off[n, k], off[n, k + 1]], axis=1))
            for i in range(2):
                part = masked(both[:, i * 128 : (i + 1) * 128], neighbors[n, k + i]).astype(jnp.bfloat16)
                scaled[n, k + i] = part
                if n >= start and k < REMOTE:
                    kept[n - start, k + i] = part

    def local_row(t, carry):
        q = start + t
        blocks, inverses, uppers = [], [], []
        for i in range(2):
            named = neighbors[q, REMOTE + i]
            place = jnp.clip(lax.rem(named, rows), 0, capacity - 1)
            blocks.append(masked(off[q, REMOTE + i], named))
            inverses.append(inverse[place])
            uppers.append(off[place, REMOTE + 1 - i])
        lowers, total = pair_sums(blocks, inverses, uppers)
        for i in range(2):
            lower[t, i] = lowers[i]
        base[t] = diag[q].astype(jnp.float32) - total
        for j in range(REMOTE):
            live = jnp.where(jnp.logical_and(levels[q] == 1, order[j] < REMOTE), neighbors[q, order[j]], -1)
            remote[j, t] = masked(off[q, order[j]], live)
        late[t] = jnp.full(late.shape[1:], levels[q].astype(jnp.float32))
        return carry

    lax.fori_loop(0, capacity, local_row, 0)

    def each(act):
        for n in range(rows):
            if n < start:
                act(pltpu.make_async_copy(scaled.at[n], factor_hbm.at[n], sems.at[0]))
                continue
            target = factor_hbm.at[n, pl.ds(REMOTE, 2)]

            @pl.when(levels[n] == 1)
            def _():
                act(pltpu.make_async_copy(lower.at[n - start], target, sems.at[1]))

            if n < capacity:

                @pl.when(levels[n] == 0)
                def _():
                    act(pltpu.make_async_copy(scaled.at[n, pl.ds(REMOTE, 2)], target, sems.at[1]))

    each(lambda c: c.start())
    each(lambda c: c.wait())


def take(capacity, t, arrived, remote, received, late, kept, total):
    order = slot_order()
    lowers, gained = pair_sums(
        [remote[j, t] for j in arrived],
        [blocks[t] for blocks in received],
        [blocks[capacity + t] for blocks in received],
    )
    is_late = late[t][:1] > 0.5
    for j, lower in zip(arrived, lowers):
        kept[t, order[j]] = jnp.where(is_late, lower, kept[t, order[j]])
    return total - gained


def early_kernel(capacity, arrived, remote, base, late, kept_in, ra, rb, total, kept):
    del kept_in
    for t in range(capacity):
        total[t] = take(capacity, t, arrived, remote, (ra, rb), late, kept, base[t])


def second_kernel(
    capacity, rows, arrived, factor_in, kept_in, inverse, total, remote, late, ra, rb, pivot, factor_hbm, kept, sem,
):
    del factor_in, kept_in
    start = rows - capacity
    pivots = [take(capacity, t, arrived, remote, (ra, rb), late, kept, total[t]) for t in range(capacity)]
    finished = kept.at[:, pl.ds(0, REMOTE)]
    copy = pltpu.make_async_copy(finished, factor_hbm.at[pl.ds(start, capacity), pl.ds(0, REMOTE)], sem)
    copy.start()
    inverses = approx_inverses(pivots, False)
    for n in range(rows):
        if n < start:
            pivot[n] = inverse[n]
            continue
        value = inverses[n - start].astype(jnp.bfloat16)
        if n < capacity:
            value = jnp.where(late[n - start][:1] > 0.5, value, inverse[n])
        pivot[n] = value
    copy.wait()


def shards(diag_blocks, off_blocks, neighbors, levels):
    rows, slots = off_blocks.shape[:2]
    size = diag_blocks.shape[1]
    capacity = 3 * rows // 4
    smem = pl.BlockSpec(memory_space=pltpu.SMEM)
    vmem = pl.BlockSpec(memory_space=pltpu.VMEM)
    hbm = pl.BlockSpec(memory_space=pltpu.HBM)
    params = pltpu.CompilerParams(vmem_limit_bytes=VMEM_LIMIT)
    bf16 = jnp.bfloat16
    payload = jax.ShapeDtypeStruct((2 * capacity, size, size), bf16)
    totals = jax.ShapeDtypeStruct((capacity, size, size), jnp.float32)
    factors = jax.ShapeDtypeStruct(off_blocks.shape, bf16)
    pivots = jax.ShapeDtypeStruct((rows, size, size), bf16)
    kepts = jax.ShapeDtypeStruct((capacity, REMOTE + 1, size, size), bf16)

    diag_blocks, off_blocks, neighbors, levels = (
        pltpu.with_memory_space_constraint(value, pltpu.HBM)
        for value in (diag_blocks, off_blocks, neighbors, levels)
    )
    *payloads, inverse, diag, off = pl.pallas_call(
        functools.partial(first_kernel, capacity, rows),
        out_shape=[payload] * REMOTE + [jax.ShapeDtypeStruct((capacity, size, size), bf16), pivots, factors],
        in_specs=[hbm] * 4,
        out_specs=[vmem] * (REMOTE + 3),
        scratch_shapes=[
            pltpu.SMEM(neighbors.shape, jnp.int32),
            pltpu.SMEM(levels.shape, jnp.int32),
            pltpu.SMEM((REMOTE * rows,), jnp.int32),
            pltpu.SemaphoreType.DMA((4 + REMOTE,)),
        ],
        compiler_params=params,
        name="first_inverses",
    )(neighbors, levels, diag_blocks, off_blocks)

    steps = transfers(lax.axis_size("row"), lax.axis_size("col"))
    received = [lax.ppermute(payloads[j], ("row", "col"), steps[j]) for j in range(REMOTE)]

    factor, base, remote, kept, late = pl.pallas_call(
        functools.partial(local_kernel, capacity, rows),
        out_shape=[
            factors,
            totals,
            jax.ShapeDtypeStruct((REMOTE, capacity, size, size), bf16),
            kepts,
            jax.ShapeDtypeStruct((capacity, 8, size), jnp.float32),
        ],
        in_specs=[smem, smem] + [vmem] * 3,
        out_specs=[hbm] + [vmem] * 4,
        scratch_shapes=[
            pltpu.VMEM((capacity, 2, size, size), bf16),
            pltpu.VMEM((capacity, slots, size, size), bf16),
            pltpu.SemaphoreType.DMA((2,)),
        ],
        compiler_params=params,
        cost_estimate=pl.CostEstimate(flops=400_000_000, bytes_accessed=4_000_000, transcendentals=0),
        name="local_slots",
    )(neighbors, levels, diag, off, inverse)

    before, after = (0, 1), (2, 3)
    total, kept = pl.pallas_call(
        functools.partial(early_kernel, capacity, before),
        out_shape=[totals, kepts],
        in_specs=[vmem] * 6,
        out_specs=[vmem, vmem],
        input_output_aliases={3: 1},
        compiler_params=params,
        name="early_slots",
    )(remote, base, late, kept, *(received[j] for j in before))

    pivot, factor, _ = pl.pallas_call(
        functools.partial(second_kernel, capacity, rows, after),
        out_shape=[pivots, factors, kepts],
        in_specs=[hbm] + [vmem] * 7,
        out_specs=[vmem, hbm, vmem],
        scratch_shapes=[pltpu.SemaphoreType.DMA],
        input_output_aliases={0: 1, 1: 2},
        compiler_params=params,
        name="second_inverses",
    )(factor, kept, inverse, total, remote, late, *(received[j] for j in after))
    return (pivot, factor)


def solution(mesh):
    in_specs = (
        P(("row", "col"), None, None),
        P(("row", "col"), None, None, None),
        P(("row", "col"), None),
        P(("row", "col")),
    )
    out_specs = (P(("row", "col"), None, None), P(("row", "col"), None, None, None))
    return jax.shard_map(shards, mesh=mesh, in_specs=in_specs, out_specs=out_specs, check_vma=False)
```

```python
import functools
import jax
import jax.numpy as jnp
from jax import lax
from jax.experimental import pallas as pl
from jax.experimental.pallas import tpu as pltpu
from jax.sharding import PartitionSpec as P

NS_STEPS = 4
MIRROR = (1, 0, 3, 2, 5, 4)
VMEM_LIMIT = 40 * 1024 * 1024
REMOTE = 4
EVERY_DEVICE = (
    ((6, 0, 2, 4), (6, 2, 3, 0), (6, 3, 2, 0), (0, 6, 3, 4)),
    ((2, 1, 0, 5), (3, 2, 0, 1), (0, 3, 2, 1), (1, 0, 3, 5)),
    ((2, 0, 1, 4), (3, 2, 1, 0), (1, 3, 0, 2), (0, 1, 4, 3)),
    ((0, 1, 2, 5), (0, 2, 3, 1), (0, 3, 1, 2), (1, 0, 5, 3)),
    ((1, 2, 4, 0), (1, 3, 2, 0), (1, 0, 3, 2), (0, 1, 4, 3)),
    ((0, 2, 5, 1), (0, 3, 2, 1), (0, 1, 3, 2), (1, 0, 5, 3)),
    ((1, 0, 2, 4), (1, 2, 3, 0), (1, 3, 2, 0), (4, 1, 3, 0)),
    ((6, 1, 2, 5), (6, 2, 3, 1), (6, 3, 2, 1), (5, 6, 3, 1)),
)
ANY_MESH = (
    ((2, 1, 3, 0), (3, 1, 2, 0)),
    ((0, 3, 2, 1), (0, 2, 3, 1)),
    ((1, 3, 2, 0), (1, 2, 3, 0)),
    ((2, 0, 3, 1), (3, 0, 2, 1)),
)


def dot(a, b):
    return jnp.dot(a, b, preferred_element_type=jnp.float32)


def dot_t(a, b):
    return lax.dot_general(a, b, (((1,), (1,)), ((), ())), preferred_element_type=jnp.float32)


def halves(value):
    high = value.astype(jnp.bfloat16)
    low = (value - high.astype(jnp.float32)).astype(jnp.bfloat16)
    return high, low


def approx_inverses(matrices, exact):
    size = matrices[0].shape[0]
    eye = (
        lax.broadcasted_iota(jnp.int32, (size, size), 0)
        == lax.broadcasted_iota(jnp.int32, (size, size), 1)
    ).astype(jnp.float32)
    iterates, residuals = [], []
    for matrix in matrices:
        turned = matrix.T
        column = jnp.max(jnp.sum(jnp.abs(matrix), axis=0, keepdims=True), axis=1, keepdims=True)
        row = jnp.max(jnp.sum(jnp.abs(turned), axis=0, keepdims=True), axis=1, keepdims=True)
        scale = 1.0 / (column * row)
        if exact:
            square = dot_t(matrix.astype(jnp.bfloat16), matrix.astype(jnp.bfloat16))
        else:
            high, low = halves(matrix)
            left = jnp.concatenate([high, low], axis=1)
            right = jnp.concatenate(
                [
                    jnp.concatenate([high, high], axis=1),
                    jnp.concatenate([low, low], axis=1),
                ],
                axis=0,
            )
            both = dot_t(left, right)
            square = both[:, :size] + both[:, size:]
        iterates.append(turned * scale)
        residuals.append(eye - square * scale)
    for step in range(NS_STEPS):
        last = step == NS_STEPS - 1
        for n in range(len(matrices)):
            r_high, r_low = halves(residuals[n])
            x_high, x_low = halves(iterates[n])
            row = jnp.concatenate([r_high, r_low], axis=1)
            right = jnp.concatenate([row, row], axis=0)
            left = jnp.concatenate([x_high, x_low], axis=1)
            if not last:
                left = jnp.concatenate([row, left], axis=0)
            both = dot(left, right)
            both = both[:, :size] + both[:, size:]
            iterates[n] = iterates[n] + both[-size:]
            if not last:
                residuals[n] = both[:size]
    return iterates


def meetings(rows, cols):
    return EVERY_DEVICE if (rows, cols) == (8, 4) else ANY_MESH


def transfers(rows, cols):
    plan = meetings(rows, cols)
    steps = [[] for _ in range(REMOTE)]
    for r in range(rows):
        for c in range(cols):
            around = ((r + 1, c), (r - 1, c), (r, c + 1), (r, c - 1), (r + 1, c), (r - 1, c), (rows - 1 - r, c))
            entry = plan[r % len(plan)][c % len(plan[0])]
            for j in range(REMOTE):
                to_row, to_col = around[entry[j]]
                if 0 <= to_row < rows and 0 <= to_col < cols:
                    steps[j].append((r * cols + c, to_row * cols + to_col))
    return steps


def slot_order():
    plan = meetings(lax.axis_size("row"), lax.axis_size("col"))
    row = lax.rem(lax.axis_index("row"), len(plan))
    col = lax.rem(lax.axis_index("col"), len(plan[0]))
    code = jnp.int32(0)
    for r, line in enumerate(plan):
        for c, entry in enumerate(line):
            packed = sum(min(entry[j], REMOTE) << (3 * j) for j in range(REMOTE))
            code = jnp.where(row * len(line) + col == r * len(line) + c, jnp.int32(packed), code)
    return tuple(lax.shift_right_logical(code, 3 * j) & 7 for j in range(REMOTE))


def masked(block, named):
    return jnp.where(named >= 0, block, jnp.zeros_like(block))


def first_kernel(
    capacity, rows, neighbors_hbm, levels_hbm, diag_hbm, off_hbm, p0, p1, p2, p3, inverse, diag, off,
    neighbors, levels, places, sems,
):
    payloads = (p0, p1, p2, p3)
    slots = slot_order()
    start = rows - capacity
    copies = [
        pltpu.make_async_copy(neighbors_hbm, neighbors, sems.at[0]),
        pltpu.make_async_copy(levels_hbm, levels, sems.at[1]),
        pltpu.make_async_copy(diag_hbm, diag, sems.at[2]),
        pltpu.make_async_copy(off_hbm, off, sems.at[3]),
    ]
    for copy in copies:
        copy.start()
    copies[0].wait()
    copies[1].wait()
    for j in range(REMOTE):
        for t in range(capacity):
            places[j * rows + t] = 0
        for n in range(capacity):
            named = neighbors[n, slots[j]]
            live = jnp.logical_and(named >= 0, levels[n] == 0)
            places[j * rows + jnp.where(live, lax.rem(named, rows) - start, capacity)] = n
    for j in range(REMOTE):
        for t in range(capacity):
            pltpu.make_async_copy(
                off_hbm.at[places[j * rows + t], slots[j]], payloads[j].at[capacity + t], sems.at[4 + j]
            ).start()
    copies[2].wait()
    inverses = approx_inverses([diag[n].astype(jnp.float32) for n in range(capacity)], True)
    for n in range(capacity):
        inverse[n] = inverses[n].astype(jnp.bfloat16)

    def pack(t, carry):
        for j in range(REMOTE):
            payloads[j][t] = inverse[places[j * rows + t]]
        return carry

    lax.fori_loop(0, capacity, pack, 0)
    copies[3].wait()
    for j in range(REMOTE):
        whole = payloads[j].at[pl.ds(capacity, capacity)]
        pltpu.make_async_copy(off_hbm.at[pl.ds(0, capacity), 0], whole, sems.at[4 + j]).wait()


def pair_sums(blocks, inverses, uppers):
    lowers = [dot(block, inverse).astype(jnp.bfloat16) for block, inverse in zip(blocks, inverses)]
    return lowers, dot(jnp.concatenate(lowers, axis=1), jnp.concatenate(uppers, axis=0))


def local_kernel(
    capacity, rows, neighbors, levels, diag, off, inverse, factor_hbm, base, remote, kept, late, lower, scaled, sems,
):
    start = rows - capacity
    slots = off.shape[1]
    order = slot_order()
    for n in range(capacity):
        for k in range(0, slots, 2):
            both = dot(inverse[n], jnp.concatenate([off[n, k], off[n, k + 1]], axis=1))
            for i in range(2):
                part = masked(both[:, i * 128 : (i + 1) * 128], neighbors[n, k + i]).astype(jnp.bfloat16)
                scaled[n, k + i] = part
                if n >= start and k < REMOTE:
                    kept[n - start, k + i] = part

    def local_row(t, carry):
        q = start + t
        blocks, inverses, uppers = [], [], []
        for i in range(2):
            named = neighbors[q, REMOTE + i]
            place = jnp.clip(lax.rem(named, rows), 0, capacity - 1)
            blocks.append(masked(off[q, REMOTE + i], named))
            inverses.append(inverse[place])
            uppers.append(off[place, REMOTE + 1 - i])
        lowers, total = pair_sums(blocks, inverses, uppers)
        for i in range(2):
            lower[t, i] = lowers[i]
        base[t] = diag[q].astype(jnp.float32) - total
        for j in range(REMOTE):
            live = jnp.where(jnp.logical_and(levels[q] == 1, order[j] < REMOTE), neighbors[q, order[j]], -1)
            remote[j, t] = masked(off[q, order[j]], live)
        late[t] = jnp.full(late.shape[1:], levels[q].astype(jnp.float32))
        return carry

    lax.fori_loop(0, capacity, local_row, 0)

    def each(act):
        for n in range(rows):
            if n < start:
                act(pltpu.make_async_copy(scaled.at[n], factor_hbm.at[n], sems.at[0]))
                continue
            target = factor_hbm.at[n, pl.ds(REMOTE, 2)]

            @pl.when(levels[n] == 1)
            def _():
                act(pltpu.make_async_copy(lower.at[n - start], target, sems.at[1]))

            if n < capacity:

                @pl.when(levels[n] == 0)
                def _():
                    act(pltpu.make_async_copy(scaled.at[n, pl.ds(REMOTE, 2)], target, sems.at[1]))

    each(lambda c: c.start())
    each(lambda c: c.wait())


def take(capacity, t, arrived, remote, received, late, kept, total):
    order = slot_order()
    lowers, gained = pair_sums(
        [remote[j, t] for j in arrived],
        [blocks[t] for blocks in received],
        [blocks[capacity + t] for blocks in received],
    )
    is_late = late[t][:1] > 0.5
    for j, lower in zip(arrived, lowers):
        kept[t, order[j]] = jnp.where(is_late, lower, kept[t, order[j]])
    return total - gained


def second_kernel(
    capacity, rows, factor_in, kept_in, inverse, base, remote, late, r0, r1, r2, r3, pivot, factor_hbm, kept, sem,
):
    del factor_in, kept_in
    start = rows - capacity
    pivots = []
    for t in range(capacity):
        left = take(capacity, t, (0, 1), remote, (r0, r1), late, kept, base[t])
        pivots.append(take(capacity, t, (2, 3), remote, (r2, r3), late, kept, left))
    finished = kept.at[:, pl.ds(0, REMOTE)]
    copy = pltpu.make_async_copy(finished, factor_hbm.at[pl.ds(start, capacity), pl.ds(0, REMOTE)], sem)
    copy.start()
    inverses = approx_inverses(pivots, False)
    for n in range(rows):
        if n < start:
            pivot[n] = inverse[n]
            continue
        value = inverses[n - start].astype(jnp.bfloat16)
        if n < capacity:
            value = jnp.where(late[n - start][:1] > 0.5, value, inverse[n])
        pivot[n] = value
    copy.wait()


def shards(diag_blocks, off_blocks, neighbors, levels):
    rows, slots = off_blocks.shape[:2]
    size = diag_blocks.shape[1]
    capacity = 3 * rows // 4
    smem = pl.BlockSpec(memory_space=pltpu.SMEM)
    vmem = pl.BlockSpec(memory_space=pltpu.VMEM)
    hbm = pl.BlockSpec(memory_space=pltpu.HBM)
    params = pltpu.CompilerParams(vmem_limit_bytes=VMEM_LIMIT)
    bf16 = jnp.bfloat16
    payload = jax.ShapeDtypeStruct((2 * capacity, size, size), bf16)
    totals = jax.ShapeDtypeStruct((capacity, size, size), jnp.float32)
    factors = jax.ShapeDtypeStruct(off_blocks.shape, bf16)
    pivots = jax.ShapeDtypeStruct((rows, size, size), bf16)
    kepts = jax.ShapeDtypeStruct((capacity, REMOTE + 1, size, size), bf16)

    diag_blocks, off_blocks, neighbors, levels = (
        pltpu.with_memory_space_constraint(value, pltpu.HBM)
        for value in (diag_blocks, off_blocks, neighbors, levels)
    )
    *payloads, inverse, diag, off = pl.pallas_call(
        functools.partial(first_kernel, capacity, rows),
        out_shape=[payload] * REMOTE + [jax.ShapeDtypeStruct((capacity, size, size), bf16), pivots, factors],
        in_specs=[hbm] * 4,
        out_specs=[vmem] * (REMOTE + 3),
        scratch_shapes=[
            pltpu.SMEM(neighbors.shape, jnp.int32),
            pltpu.SMEM(levels.shape, jnp.int32),
            pltpu.SMEM((REMOTE * rows,), jnp.int32),
            pltpu.SemaphoreType.DMA((4 + REMOTE,)),
        ],
        compiler_params=params,
        name="first_inverses",
    )(neighbors, levels, diag_blocks, off_blocks)

    steps = transfers(lax.axis_size("row"), lax.axis_size("col"))
    received = [lax.ppermute(payloads[j], ("row", "col"), steps[j]) for j in range(REMOTE)]

    factor, base, remote, kept, late = pl.pallas_call(
        functools.partial(local_kernel, capacity, rows),
        out_shape=[
            factors,
            totals,
            jax.ShapeDtypeStruct((REMOTE, capacity, size, size), bf16),
            kepts,
            jax.ShapeDtypeStruct((capacity, 8, size), jnp.float32),
        ],
        in_specs=[smem, smem] + [vmem] * 3,
        out_specs=[hbm] + [vmem] * 4,
        scratch_shapes=[
            pltpu.VMEM((capacity, 2, size, size), bf16),
            pltpu.VMEM((capacity, slots, size, size), bf16),
            pltpu.SemaphoreType.DMA((2,)),
        ],
        compiler_params=params,
        cost_estimate=pl.CostEstimate(flops=400_000_000, bytes_accessed=4_000_000, transcendentals=0),
        name="local_slots",
    )(neighbors, levels, diag, off, inverse)

    pivot, factor, _ = pl.pallas_call(
        functools.partial(second_kernel, capacity, rows),
        out_shape=[pivots, factors, kepts],
        in_specs=[hbm] + [vmem] * 9,
        out_specs=[vmem, hbm, vmem],
        scratch_shapes=[pltpu.SemaphoreType.DMA],
        input_output_aliases={0: 1, 1: 2},
        compiler_params=params,
        name="second_inverses",
    )(factor, kept, inverse, base, remote, late, *received)
    return (pivot, factor)


def solution(mesh):
    in_specs = (
        P(("row", "col"), None, None),
        P(("row", "col"), None, None, None),
        P(("row", "col"), None),
        P(("row", "col")),
    )
    out_specs = (P(("row", "col"), None, None), P(("row", "col"), None, None, None))
    return jax.shard_map(shards, mesh=mesh, in_specs=in_specs, out_specs=out_specs, check_vma=False)
```

```python
import functools
import jax
import jax.numpy as jnp
from jax import lax
from jax.experimental import pallas as pl
from jax.experimental.pallas import tpu as pltpu
from jax.sharding import PartitionSpec as P

NS_STEPS = 4
MIRROR = (1, 0, 3, 2, 5, 4)
VMEM_LIMIT = 40 * 1024 * 1024
REMOTE = 4
EVERY_DEVICE = (
    ((6, 0, 4, 2), (6, 2, 0, 3), (6, 3, 2, 0), (0, 6, 3, 4)),
    ((2, 1, 5, 0), (3, 2, 1, 0), (0, 3, 2, 1), (1, 0, 3, 5)),
    ((2, 4, 0, 1), (3, 2, 0, 1), (1, 3, 2, 0), (0, 1, 3, 4)),
    ((0, 5, 1, 2), (0, 2, 1, 3), (0, 3, 2, 1), (1, 0, 3, 5)),
    ((1, 2, 4, 0), (1, 3, 2, 0), (1, 0, 3, 2), (0, 1, 4, 3)),
    ((0, 2, 5, 1), (0, 3, 2, 1), (0, 1, 3, 2), (1, 0, 5, 3)),
    ((1, 4, 2, 0), (1, 2, 3, 0), (1, 3, 0, 2), (4, 1, 0, 3)),
    ((6, 5, 2, 1), (6, 2, 3, 1), (6, 3, 1, 2), (5, 6, 1, 3)),
)
ANY_MESH = (
    ((2, 1, 3, 0), (3, 1, 2, 0)),
    ((0, 3, 2, 1), (0, 2, 3, 1)),
    ((1, 3, 2, 0), (1, 2, 3, 0)),
    ((2, 0, 3, 1), (3, 0, 2, 1)),
)


def dot(a, b):
    return jnp.dot(a, b, preferred_element_type=jnp.float32)


def dot_t(a, b):
    return lax.dot_general(a, b, (((1,), (1,)), ((), ())), preferred_element_type=jnp.float32)


def halves(value):
    high = value.astype(jnp.bfloat16)
    low = (value - high.astype(jnp.float32)).astype(jnp.bfloat16)
    return high, low


def approx_inverses(matrices, exact):
    size = matrices[0].shape[0]
    eye = (
        lax.broadcasted_iota(jnp.int32, (size, size), 0)
        == lax.broadcasted_iota(jnp.int32, (size, size), 1)
    ).astype(jnp.float32)
    iterates, residuals = [], []
    for matrix in matrices:
        turned = matrix.T
        column = jnp.max(jnp.sum(jnp.abs(matrix), axis=0, keepdims=True), axis=1, keepdims=True)
        row = jnp.max(jnp.sum(jnp.abs(turned), axis=0, keepdims=True), axis=1, keepdims=True)
        scale = 1.0 / (column * row)
        if exact:
            square = dot_t(matrix.astype(jnp.bfloat16), matrix.astype(jnp.bfloat16))
        else:
            high, low = halves(matrix)
            left = jnp.concatenate([high, low], axis=1)
            right = jnp.concatenate(
                [
                    jnp.concatenate([high, high], axis=1),
                    jnp.concatenate([low, low], axis=1),
                ],
                axis=0,
            )
            both = dot_t(left, right)
            square = both[:, :size] + both[:, size:]
        iterates.append(turned * scale)
        residuals.append(eye - square * scale)
    for step in range(NS_STEPS):
        last = step == NS_STEPS - 1
        for n in range(len(matrices)):
            r_high, r_low = halves(residuals[n])
            x_high, x_low = halves(iterates[n])
            row = jnp.concatenate([r_high, r_low], axis=1)
            right = jnp.concatenate([row, row], axis=0)
            left = jnp.concatenate([x_high, x_low], axis=1)
            if not last:
                left = jnp.concatenate([row, left], axis=0)
            both = dot(left, right)
            both = both[:, :size] + both[:, size:]
            iterates[n] = iterates[n] + both[-size:]
            if not last:
                residuals[n] = both[:size]
    return iterates


def meetings(rows, cols):
    return EVERY_DEVICE if (rows, cols) == (8, 4) else ANY_MESH


def transfers(rows, cols):
    plan = meetings(rows, cols)
    steps = [[] for _ in range(REMOTE)]
    for r in range(rows):
        for c in range(cols):
            around = ((r + 1, c), (r - 1, c), (r, c + 1), (r, c - 1), (r + 1, c), (r - 1, c), (rows - 1 - r, c))
            entry = plan[r % len(plan)][c % len(plan[0])]
            for j in range(REMOTE):
                to_row, to_col = around[entry[j]]
                if 0 <= to_row < rows and 0 <= to_col < cols:
                    steps[j].append((r * cols + c, to_row * cols + to_col))
    return steps


def slot_order():
    plan = meetings(lax.axis_size("row"), lax.axis_size("col"))
    row = lax.rem(lax.axis_index("row"), len(plan))
    col = lax.rem(lax.axis_index("col"), len(plan[0]))
    code = jnp.int32(0)
    for r, line in enumerate(plan):
        for c, entry in enumerate(line):
            packed = sum(min(entry[j], REMOTE) << (3 * j) for j in range(REMOTE))
            code = jnp.where(row * len(line) + col == r * len(line) + c, jnp.int32(packed), code)
    return tuple(lax.shift_right_logical(code, 3 * j) & 7 for j in range(REMOTE))


def masked(block, named):
    return jnp.where(named >= 0, block, jnp.zeros_like(block))


def first_kernel(
    capacity, rows, neighbors_hbm, levels_hbm, diag_hbm, off_hbm, p0, p1, p2, p3, inverse, diag, off,
    neighbors, levels, places, sems,
):
    payloads = (p0, p1, p2, p3)
    slots = slot_order()
    start = rows - capacity
    copies = [
        pltpu.make_async_copy(neighbors_hbm, neighbors, sems.at[0]),
        pltpu.make_async_copy(levels_hbm, levels, sems.at[1]),
        pltpu.make_async_copy(diag_hbm, diag, sems.at[2]),
        pltpu.make_async_copy(off_hbm, off, sems.at[3]),
    ]
    for copy in copies:
        copy.start()
    copies[0].wait()
    copies[1].wait()
    for j in range(REMOTE):
        for t in range(capacity):
            places[j * rows + t] = 0
        for n in range(capacity):
            named = neighbors[n, slots[j]]
            live = jnp.logical_and(named >= 0, levels[n] == 0)
            places[j * rows + jnp.where(live, lax.rem(named, rows) - start, capacity)] = n
    for j in range(REMOTE):
        for t in range(capacity):
            pltpu.make_async_copy(
                off_hbm.at[places[j * rows + t], slots[j]], payloads[j].at[capacity + t], sems.at[4 + j]
            ).start()
    copies[2].wait()
    inverses = approx_inverses([diag[n].astype(jnp.float32) for n in range(capacity)], True)
    for n in range(capacity):
        inverse[n] = inverses[n].astype(jnp.bfloat16)

    def pack(t, carry):
        for j in range(REMOTE):
            payloads[j][t] = inverse[places[j * rows + t]]
        return carry

    lax.fori_loop(0, capacity, pack, 0)
    copies[3].wait()
    for j in range(REMOTE):
        whole = payloads[j].at[pl.ds(capacity, capacity)]
        pltpu.make_async_copy(off_hbm.at[pl.ds(0, capacity), 0], whole, sems.at[4 + j]).wait()


def pair_sums(blocks, inverses, uppers):
    lowers = [dot(block, inverse).astype(jnp.bfloat16) for block, inverse in zip(blocks, inverses)]
    return lowers, dot(jnp.concatenate(lowers, axis=1), jnp.concatenate(uppers, axis=0))


def local_kernel(
    capacity, rows, neighbors, levels, diag, off, inverse, factor_hbm, base, remote, kept, late, lower, scaled, sems,
):
    start = rows - capacity
    slots = off.shape[1]
    order = slot_order()
    for n in range(capacity):
        for k in range(0, slots, 2):
            both = dot(inverse[n], jnp.concatenate([off[n, k], off[n, k + 1]], axis=1))
            for i in range(2):
                part = masked(both[:, i * 128 : (i + 1) * 128], neighbors[n, k + i]).astype(jnp.bfloat16)
                scaled[n, k + i] = part
                if n >= start and k < REMOTE:
                    kept[n - start, k + i] = part

    def local_row(t, carry):
        q = start + t
        blocks, inverses, uppers = [], [], []
        for i in range(2):
            named = neighbors[q, REMOTE + i]
            place = jnp.clip(lax.rem(named, rows), 0, capacity - 1)
            blocks.append(masked(off[q, REMOTE + i], named))
            inverses.append(inverse[place])
            uppers.append(off[place, REMOTE + 1 - i])
        lowers, total = pair_sums(blocks, inverses, uppers)
        for i in range(2):
            lower[t, i] = lowers[i]
        base[t] = diag[q].astype(jnp.float32) - total
        for j in range(REMOTE):
            live = jnp.where(jnp.logical_and(levels[q] == 1, order[j] < REMOTE), neighbors[q, order[j]], -1)
            remote[j, t] = masked(off[q, order[j]], live)
        late[t] = jnp.full(late.shape[1:], levels[q].astype(jnp.float32))
        return carry

    lax.fori_loop(0, capacity, local_row, 0)

    def each(act):
        for n in range(rows):
            if n < start:
                act(pltpu.make_async_copy(scaled.at[n], factor_hbm.at[n], sems.at[0]))
                continue
            target = factor_hbm.at[n, pl.ds(REMOTE, 2)]

            @pl.when(levels[n] == 1)
            def _():
                act(pltpu.make_async_copy(lower.at[n - start], target, sems.at[1]))

            if n < capacity:

                @pl.when(levels[n] == 0)
                def _():
                    act(pltpu.make_async_copy(scaled.at[n, pl.ds(REMOTE, 2)], target, sems.at[1]))

    each(lambda c: c.start())
    each(lambda c: c.wait())


def take(capacity, t, arrived, remote, received, late, kept, total):
    order = slot_order()
    lowers, gained = pair_sums(
        [remote[j, t] for j in arrived],
        [blocks[t] for blocks in received],
        [blocks[capacity + t] for blocks in received],
    )
    is_late = late[t][:1] > 0.5
    for j, lower in zip(arrived, lowers):
        kept[t, order[j]] = jnp.where(is_late, lower, kept[t, order[j]])
    return total - gained


def second_kernel(
    capacity, rows, factor_in, kept_in, inverse, base, remote, late, r0, r1, r2, r3, pivot, factor_hbm, kept, sem,
):
    del factor_in, kept_in
    start = rows - capacity
    pivots = []
    for t in range(capacity):
        left = take(capacity, t, (0, 1), remote, (r0, r1), late, kept, base[t])
        pivots.append(take(capacity, t, (2, 3), remote, (r2, r3), late, kept, left))
    finished = kept.at[:, pl.ds(0, REMOTE)]
    copy = pltpu.make_async_copy(finished, factor_hbm.at[pl.ds(start, capacity), pl.ds(0, REMOTE)], sem)
    copy.start()
    inverses = approx_inverses(pivots, False)
    for n in range(rows):
        if n < start:
            pivot[n] = inverse[n]
            continue
        value = inverses[n - start].astype(jnp.bfloat16)
        if n < capacity:
            value = jnp.where(late[n - start][:1] > 0.5, value, inverse[n])
        pivot[n] = value
    copy.wait()


def shards(diag_blocks, off_blocks, neighbors, levels):
    rows, slots = off_blocks.shape[:2]
    size = diag_blocks.shape[1]
    capacity = 3 * rows // 4
    smem = pl.BlockSpec(memory_space=pltpu.SMEM)
    vmem = pl.BlockSpec(memory_space=pltpu.VMEM)
    hbm = pl.BlockSpec(memory_space=pltpu.HBM)
    params = pltpu.CompilerParams(vmem_limit_bytes=VMEM_LIMIT)
    bf16 = jnp.bfloat16
    payload = jax.ShapeDtypeStruct((2 * capacity, size, size), bf16)
    totals = jax.ShapeDtypeStruct((capacity, size, size), jnp.float32)
    factors = jax.ShapeDtypeStruct(off_blocks.shape, bf16)
    pivots = jax.ShapeDtypeStruct((rows, size, size), bf16)
    kepts = jax.ShapeDtypeStruct((capacity, REMOTE + 1, size, size), bf16)

    diag_blocks, off_blocks, neighbors, levels = (
        pltpu.with_memory_space_constraint(value, pltpu.HBM)
        for value in (diag_blocks, off_blocks, neighbors, levels)
    )
    *payloads, inverse, diag, off = pl.pallas_call(
        functools.partial(first_kernel, capacity, rows),
        out_shape=[payload] * REMOTE + [jax.ShapeDtypeStruct((capacity, size, size), bf16), pivots, factors],
        in_specs=[hbm] * 4,
        out_specs=[vmem] * (REMOTE + 3),
        scratch_shapes=[
            pltpu.SMEM(neighbors.shape, jnp.int32),
            pltpu.SMEM(levels.shape, jnp.int32),
            pltpu.SMEM((REMOTE * rows,), jnp.int32),
            pltpu.SemaphoreType.DMA((4 + REMOTE,)),
        ],
        compiler_params=params,
        name="first_inverses",
    )(neighbors, levels, diag_blocks, off_blocks)

    steps = transfers(lax.axis_size("row"), lax.axis_size("col"))
    received = [lax.ppermute(payloads[j], ("row", "col"), steps[j]) for j in range(REMOTE)]

    factor, base, remote, kept, late = pl.pallas_call(
        functools.partial(local_kernel, capacity, rows),
        out_shape=[
            factors,
            totals,
            jax.ShapeDtypeStruct((REMOTE, capacity, size, size), bf16),
            kepts,
            jax.ShapeDtypeStruct((capacity, 8, size), jnp.float32),
        ],
        in_specs=[smem, smem] + [vmem] * 3,
        out_specs=[hbm] + [vmem] * 4,
        scratch_shapes=[
            pltpu.VMEM((capacity, 2, size, size), bf16),
            pltpu.VMEM((capacity, slots, size, size), bf16),
            pltpu.SemaphoreType.DMA((2,)),
        ],
        compiler_params=params,
        cost_estimate=pl.CostEstimate(flops=400_000_000, bytes_accessed=4_000_000, transcendentals=0),
        name="local_slots",
    )(neighbors, levels, diag, off, inverse)

    pivot, factor, _ = pl.pallas_call(
        functools.partial(second_kernel, capacity, rows),
        out_shape=[pivots, factors, kepts],
        in_specs=[hbm] + [vmem] * 9,
        out_specs=[vmem, hbm, vmem],
        scratch_shapes=[pltpu.SemaphoreType.DMA],
        input_output_aliases={0: 1, 1: 2},
        compiler_params=params,
        name="second_inverses",
    )(factor, kept, inverse, base, remote, late, *received)
    return (pivot, factor)


def solution(mesh):
    in_specs = (
        P(("row", "col"), None, None),
        P(("row", "col"), None, None, None),
        P(("row", "col"), None),
        P(("row", "col")),
    )
    out_specs = (P(("row", "col"), None, None), P(("row", "col"), None, None, None))
    return jax.shard_map(shards, mesh=mesh, in_specs=in_specs, out_specs=out_specs, check_vma=False)
```

```python
import functools
import jax
import jax.numpy as jnp
from jax import lax
from jax.experimental import pallas as pl
from jax.experimental.pallas import tpu as pltpu
from jax.sharding import PartitionSpec as P

NS_STEPS = 4
MIRROR = (1, 0, 3, 2, 5, 4)
VMEM_LIMIT = 40 * 1024 * 1024
REMOTE = 4
EVERY_DEVICE = (
    ((6, 0, 4, 2), (6, 2, 0, 3), (6, 3, 2, 0), (0, 6, 3, 4)),
    ((2, 1, 5, 0), (3, 2, 1, 0), (0, 3, 2, 1), (1, 0, 3, 5)),
    ((2, 4, 0, 1), (3, 2, 0, 1), (1, 3, 2, 0), (0, 1, 3, 4)),
    ((0, 5, 1, 2), (0, 2, 1, 3), (0, 3, 2, 1), (1, 0, 3, 5)),
    ((1, 2, 4, 0), (1, 3, 2, 0), (1, 0, 3, 2), (0, 1, 4, 3)),
    ((0, 2, 5, 1), (0, 3, 2, 1), (0, 1, 3, 2), (1, 0, 5, 3)),
    ((1, 4, 2, 0), (1, 2, 3, 0), (1, 3, 0, 2), (4, 1, 0, 3)),
    ((6, 5, 2, 1), (6, 2, 3, 1), (6, 3, 1, 2), (5, 6, 1, 3)),
)
ANY_MESH = (
    ((2, 1, 3, 0), (3, 1, 2, 0)),
    ((0, 3, 2, 1), (0, 2, 3, 1)),
    ((1, 3, 2, 0), (1, 2, 3, 0)),
    ((2, 0, 3, 1), (3, 0, 2, 1)),
)


def dot(a, b):
    return jnp.dot(a, b, preferred_element_type=jnp.float32)


def dot_t(a, b):
    return lax.dot_general(a, b, (((1,), (1,)), ((), ())), preferred_element_type=jnp.float32)


def halves(value):
    high = value.astype(jnp.bfloat16)
    low = (value - high.astype(jnp.float32)).astype(jnp.bfloat16)
    return high, low


def approx_inverses(matrices, exact):
    size = matrices[0].shape[0]
    eye = (
        lax.broadcasted_iota(jnp.int32, (size, size), 0)
        == lax.broadcasted_iota(jnp.int32, (size, size), 1)
    ).astype(jnp.float32)
    iterates, residuals = [], []
    for matrix in matrices:
        turned = matrix.T
        column = jnp.max(jnp.sum(jnp.abs(matrix), axis=0, keepdims=True), axis=1, keepdims=True)
        row = jnp.max(jnp.sum(jnp.abs(turned), axis=0, keepdims=True), axis=1, keepdims=True)
        scale = 1.0 / (column * row)
        if exact:
            square = dot_t(matrix.astype(jnp.bfloat16), matrix.astype(jnp.bfloat16))
        else:
            high, low = halves(matrix)
            left = jnp.concatenate([high, low], axis=1)
            right = jnp.concatenate(
                [
                    jnp.concatenate([high, high], axis=1),
                    jnp.concatenate([low, low], axis=1),
                ],
                axis=0,
            )
            both = dot_t(left, right)
            square = both[:, :size] + both[:, size:]
        iterates.append(turned * scale)
        residuals.append(eye - square * scale)
    for step in range(NS_STEPS):
        last = step == NS_STEPS - 1
        for n in range(len(matrices)):
            r_high, r_low = halves(residuals[n])
            x_high, x_low = halves(iterates[n])
            row = jnp.concatenate([r_high, r_low], axis=1)
            right = jnp.concatenate([row, row], axis=0)
            left = jnp.concatenate([x_high, x_low], axis=1)
            if not last:
                left = jnp.concatenate([row, left], axis=0)
            both = dot(left, right)
            both = both[:, :size] + both[:, size:]
            iterates[n] = iterates[n] + both[-size:]
            if not last:
                residuals[n] = both[:size]
    return iterates


def meetings(rows, cols):
    return EVERY_DEVICE if (rows, cols) == (8, 4) else ANY_MESH


def transfers(rows, cols):
    plan = meetings(rows, cols)
    steps = [[] for _ in range(REMOTE)]
    for r in range(rows):
        for c in range(cols):
            around = ((r + 1, c), (r - 1, c), (r, c + 1), (r, c - 1), (r + 1, c), (r - 1, c), (rows - 1 - r, c))
            entry = plan[r % len(plan)][c % len(plan[0])]
            for j in range(REMOTE):
                to_row, to_col = around[entry[j]]
                if 0 <= to_row < rows and 0 <= to_col < cols:
                    steps[j].append((r * cols + c, to_row * cols + to_col))
    return steps


def slot_order():
    plan = meetings(lax.axis_size("row"), lax.axis_size("col"))
    row = lax.rem(lax.axis_index("row"), len(plan))
    col = lax.rem(lax.axis_index("col"), len(plan[0]))
    code = jnp.int32(0)
    for r, line in enumerate(plan):
        for c, entry in enumerate(line):
            packed = sum(min(entry[j], REMOTE) << (3 * j) for j in range(REMOTE))
            code = jnp.where(row * len(line) + col == r * len(line) + c, jnp.int32(packed), code)
    return tuple(lax.shift_right_logical(code, 3 * j) & 7 for j in range(REMOTE))


def masked(block, named):
    return jnp.where(named >= 0, block, jnp.zeros_like(block))


def first_kernel(
    capacity, rows, neighbors_hbm, levels_hbm, diag_hbm, off_hbm, p0, p1, p2, p3, inverse, diag, off,
    neighbors, levels, places, sems,
):
    payloads = (p0, p1, p2, p3)
    slots = slot_order()
    start = rows - capacity
    copies = [
        pltpu.make_async_copy(neighbors_hbm, neighbors, sems.at[0]),
        pltpu.make_async_copy(levels_hbm, levels, sems.at[1]),
        pltpu.make_async_copy(diag_hbm, diag, sems.at[2]),
        pltpu.make_async_copy(off_hbm, off, sems.at[3]),
    ]
    for copy in copies:
        copy.start()
    copies[0].wait()
    copies[1].wait()
    for j in range(REMOTE):
        for t in range(capacity):
            places[j * rows + t] = 0
        for n in range(capacity):
            named = neighbors[n, slots[j]]
            live = jnp.logical_and(named >= 0, levels[n] == 0)
            places[j * rows + jnp.where(live, lax.rem(named, rows) - start, capacity)] = n
    for j in range(REMOTE):
        for t in range(capacity):
            pltpu.make_async_copy(
                off_hbm.at[places[j * rows + t], slots[j]], payloads[j].at[capacity + t], sems.at[4 + j]
            ).start()
    copies[2].wait()
    inverses = approx_inverses([diag[n].astype(jnp.float32) for n in range(capacity)], True)
    for n in range(capacity):
        inverse[n] = inverses[n].astype(jnp.bfloat16)

    def pack(t, carry):
        for j in range(REMOTE):
            payloads[j][t] = inverse[places[j * rows + t]]
        return carry

    lax.fori_loop(0, capacity, pack, 0)
    copies[3].wait()
    for j in range(REMOTE):
        whole = payloads[j].at[pl.ds(capacity, capacity)]
        pltpu.make_async_copy(off_hbm.at[pl.ds(0, capacity), 0], whole, sems.at[4 + j]).wait()


def pair_sums(blocks, inverses, uppers):
    lowers = [dot(block, inverse).astype(jnp.bfloat16) for block, inverse in zip(blocks, inverses)]
    return lowers, dot(jnp.concatenate(lowers, axis=1), jnp.concatenate(uppers, axis=0))


def local_kernel(
    capacity, rows, neighbors, levels, diag, off, inverse, factor_hbm, base, remote, kept, late, lower, scaled, sems,
):
    start = rows - capacity
    slots = off.shape[1]
    order = slot_order()
    for n in range(capacity):
        for k in range(0, slots, 2):
            both = dot(inverse[n], jnp.concatenate([off[n, k], off[n, k + 1]], axis=1))
            for i in range(2):
                part = masked(both[:, i * 128 : (i + 1) * 128], neighbors[n, k + i]).astype(jnp.bfloat16)
                scaled[n, k + i] = part
                if n >= start and k < REMOTE:
                    kept[n - start, k + i] = part

    def local_row(t, carry):
        q = start + t
        blocks, inverses, uppers = [], [], []
        for i in range(2):
            named = neighbors[q, REMOTE + i]
            place = jnp.clip(lax.rem(named, rows), 0, capacity - 1)
            blocks.append(masked(off[q, REMOTE + i], named))
            inverses.append(inverse[place])
            uppers.append(off[place, REMOTE + 1 - i])
        lowers, total = pair_sums(blocks, inverses, uppers)
        for i in range(2):
            lower[t, i] = lowers[i]
        base[t] = diag[q].astype(jnp.float32) - total
        for j in range(REMOTE):
            live = jnp.where(jnp.logical_and(levels[q] == 1, order[j] < REMOTE), neighbors[q, order[j]], -1)
            remote[j, t] = masked(off[q, order[j]], live)
        late[t] = jnp.full(late.shape[1:], levels[q].astype(jnp.float32))
        return carry

    lax.fori_loop(0, capacity, local_row, 0)

    def each(act):
        for n in range(rows):
            if n < start:
                act(pltpu.make_async_copy(scaled.at[n], factor_hbm.at[n], sems.at[0]))
                continue
            target = factor_hbm.at[n, pl.ds(REMOTE, 2)]

            @pl.when(levels[n] == 1)
            def _():
                act(pltpu.make_async_copy(lower.at[n - start], target, sems.at[1]))

            if n < capacity:

                @pl.when(levels[n] == 0)
                def _():
                    act(pltpu.make_async_copy(scaled.at[n, pl.ds(REMOTE, 2)], target, sems.at[1]))

    each(lambda c: c.start())
    each(lambda c: c.wait())


def take(capacity, order, t, arrived, remote, received, late, kept, total):
    lowers, gained = pair_sums(
        [remote[j, t] for j in arrived],
        [blocks[t] for blocks in received],
        [blocks[capacity + t] for blocks in received],
    )
    is_late = late[t][:1] > 0.5
    for j, lower in zip(arrived, lowers):
        kept[t, order[j]] = jnp.where(is_late, lower, kept[t, order[j]])
    return total - gained


def second_kernel(
    capacity, rows, factor_in, kept_in, inverse, base, remote, late, r0, r1, r2, r3, pivot, factor_hbm, kept, sem,
):
    del factor_in, kept_in
    start = rows - capacity
    order = slot_order()
    pivots = []
    for t in range(capacity):
        left = take(capacity, order, t, (0, 1), remote, (r0, r1), late, kept, base[t])
        pivots.append(take(capacity, order, t, (2, 3), remote, (r2, r3), late, kept, left))
    finished = kept.at[:, pl.ds(0, REMOTE)]
    copy = pltpu.make_async_copy(finished, factor_hbm.at[pl.ds(start, capacity), pl.ds(0, REMOTE)], sem)
    copy.start()
    inverses = approx_inverses(pivots, False)
    for n in range(rows):
        if n < start:
            pivot[n] = inverse[n]
            continue
        value = inverses[n - start].astype(jnp.bfloat16)
        if n < capacity:
            value = jnp.where(late[n - start][:1] > 0.5, value, inverse[n])
        pivot[n] = value
    copy.wait()


def shards(diag_blocks, off_blocks, neighbors, levels):
    rows, slots = off_blocks.shape[:2]
    size = diag_blocks.shape[1]
    capacity = 3 * rows // 4
    smem = pl.BlockSpec(memory_space=pltpu.SMEM)
    vmem = pl.BlockSpec(memory_space=pltpu.VMEM)
    hbm = pl.BlockSpec(memory_space=pltpu.HBM)
    params = pltpu.CompilerParams(vmem_limit_bytes=VMEM_LIMIT)
    bf16 = jnp.bfloat16
    payload = jax.ShapeDtypeStruct((2 * capacity, size, size), bf16)
    totals = jax.ShapeDtypeStruct((capacity, size, size), jnp.float32)
    factors = jax.ShapeDtypeStruct(off_blocks.shape, bf16)
    pivots = jax.ShapeDtypeStruct((rows, size, size), bf16)
    kepts = jax.ShapeDtypeStruct((capacity, REMOTE + 1, size, size), bf16)

    diag_blocks, off_blocks, neighbors, levels = (
        pltpu.with_memory_space_constraint(value, pltpu.HBM)
        for value in (diag_blocks, off_blocks, neighbors, levels)
    )
    *payloads, inverse, diag, off = pl.pallas_call(
        functools.partial(first_kernel, capacity, rows),
        out_shape=[payload] * REMOTE + [jax.ShapeDtypeStruct((capacity, size, size), bf16), pivots, factors],
        in_specs=[hbm] * 4,
        out_specs=[vmem] * (REMOTE + 3),
        scratch_shapes=[
            pltpu.SMEM(neighbors.shape, jnp.int32),
            pltpu.SMEM(levels.shape, jnp.int32),
            pltpu.SMEM((REMOTE * rows,), jnp.int32),
            pltpu.SemaphoreType.DMA((4 + REMOTE,)),
        ],
        compiler_params=params,
        name="first_inverses",
    )(neighbors, levels, diag_blocks, off_blocks)

    steps = transfers(lax.axis_size("row"), lax.axis_size("col"))
    received = [lax.ppermute(payloads[j], ("row", "col"), steps[j]) for j in range(REMOTE)]

    factor, base, remote, kept, late = pl.pallas_call(
        functools.partial(local_kernel, capacity, rows),
        out_shape=[
            factors,
            totals,
            jax.ShapeDtypeStruct((REMOTE, capacity, size, size), bf16),
            kepts,
            jax.ShapeDtypeStruct((capacity, 8, size), jnp.float32),
        ],
        in_specs=[smem, smem] + [vmem] * 3,
        out_specs=[hbm] + [vmem] * 4,
        scratch_shapes=[
            pltpu.VMEM((capacity, 2, size, size), bf16),
            pltpu.VMEM((capacity, slots, size, size), bf16),
            pltpu.SemaphoreType.DMA((2,)),
        ],
        compiler_params=params,
        cost_estimate=pl.CostEstimate(flops=400_000_000, bytes_accessed=4_000_000, transcendentals=0),
        name="local_slots",
    )(neighbors, levels, diag, off, inverse)

    pivot, factor, _ = pl.pallas_call(
        functools.partial(second_kernel, capacity, rows),
        out_shape=[pivots, factors, kepts],
        in_specs=[hbm] + [vmem] * 9,
        out_specs=[vmem, hbm, vmem],
        scratch_shapes=[pltpu.SemaphoreType.DMA],
        input_output_aliases={0: 1, 1: 2},
        compiler_params=params,
        name="second_inverses",
    )(factor, kept, inverse, base, remote, late, *received)
    return (pivot, factor)


def solution(mesh):
    in_specs = (
        P(("row", "col"), None, None),
        P(("row", "col"), None, None, None),
        P(("row", "col"), None),
        P(("row", "col")),
    )
    out_specs = (P(("row", "col"), None, None), P(("row", "col"), None, None, None))
    return jax.shard_map(shards, mesh=mesh, in_specs=in_specs, out_specs=out_specs, check_vma=False)
```
